128 devices in a mesh: section: 4 (over z), ctx: 16 (over x_hi, y, core), mirror: 2 (over x_lo).
Axes of the slice: x: 4 (x_hi: 2, x_lo: 2; x = x_hi * 2 + x_lo), y: 4, z: 4, core: 2. Of those that a mesh axis runs over, the one named last changes fastest.
Arguments:
- queries: bfloat16 [4, 2, 4096, 2048], P('section', 'mirror', 'ctx'), may hold values from -480 to 480
- saved_keys: bfloat16 [4, 2, 4096, 1024], P('section', 'mirror', 'ctx'), may hold values from -6 to 6
- saved_values: bfloat16 [4, 2, 4096, 1024], P('section', 'mirror', 'ctx'), may hold values from -6 to 6
- output_gradient: bfloat16 [4, 2, 4096, 2048], P('section', 'mirror', 'ctx'), may hold values from -96 to 96
- layer_input: bfloat16 [4, 2, 4096, 4608], P('section', 'mirror', 'ctx'), may hold values from -0.375 to 0.375
- hadamard_signs: int32 [4, 1024], replicated, may hold values from -1 to 1, as said below
Outputs:
- query_gradient: bfloat16 [4, 2, 4096, 2048], P('section', 'mirror', 'ctx')
- key_gradient: bfloat16 [4, 2, 4096, 1024], P('section', 'mirror', 'ctx')
- value_gradient: bfloat16 [4, 2, 4096, 1024], P('section', 'mirror', 'ctx')
- rotated_grad: float32 [4, 4608, 1024], P('section', ('ctx', 'mirror'))
The draws below stay inside these ranges and needn't reach their ends.
Inputs may be any that keep to these rules, and one draw needn't show every extreme that they name: `hadamard_signs`: every entry is -1 or +1.
All inputs are finite; a program needn't handle non-finite values.
Results may differ from the reference program's by a relative error of at most 0.022.
Values may be sent and summed in bfloat16 or wider, within the bound.
No kernel may reach another device: no remote copies, remote signals or barrier semaphores. Data moves between devices by JAX's collectives and lax.ppermute only.
A program may use at most 192 MiB of HBM per device.

```python
import math
import jax
import jax.numpy as jnp
from jax import lax

D = 4608
QUERY_HEADS = 16
KEY_VALUE_HEADS = 8
HEAD_SIZE = 128
WINDOW = 2048
ROWS = 256
SEQUENCE_LENGTH = 4096
N_SECTION = 4
N_MIRROR = 2


def draw_hadamard_signs(key, part):
    key = jax.random.fold_in(key, 7)
    random_signs = jax.random.randint(key, (N_SECTION, KEY_VALUE_HEADS * HEAD_SIZE), 0, 2)
    return (2 * random_signs - 1).astype(jnp.int32)


def draw_queries(key, part):
    key = jax.random.fold_in(key, 11)
    base_key, pick_key, factor_key = jax.random.split(key, 3)
    full_shape = (N_SECTION, N_MIRROR, SEQUENCE_LENGTH, QUERY_HEADS * HEAD_SIZE)
    row_shape = (N_SECTION, N_MIRROR, SEQUENCE_LENGTH, 1)
    base = jax.random.truncated_normal(base_key, -6.0, 6.0, full_shape, jnp.float32)
    picked = jax.random.uniform(pick_key, row_shape, jnp.float32) < 0.1
    factor = jnp.exp(jax.random.uniform(factor_key, row_shape, jnp.float32, math.log(40.0), math.log(80.0)))
    return (base * jnp.where(picked, factor, 1.0)).astype(jnp.bfloat16)


def block_levels(key, dims, pieces, low, high):
    loudness = 1.0
    for dim, shards_of in pieces:
        heights = jax.random.uniform(jax.random.fold_in(jax.random.fold_in(key, 6), dim), (shards_of,), jnp.float32, low / len(pieces), high / len(pieces))
        loudness = loudness * jnp.repeat(jnp.exp(heights), dims[dim] // shards_of).reshape((-1,) + (1,) * (len(dims) - 1 - dim))
    return loudness


def noise(stream_key, shape, spread, limit, shards=(), kind=jnp.bfloat16):
    values = jax.random.normal(stream_key, shape, jnp.float32) * spread
    if len(shards) > 0:
        values = block_levels(stream_key, shape, shards, -0.22, 0.18) * values
    return jnp.clip(values, min=-limit, max=limit).astype(kind)


def setup_inputs(seed: int = 0) -> dict:
    splits = jax.random.split(jax.random.key(seed), 7)
    queries = draw_queries(jax.random.fold_in(splits[6], 71), 0)
    saved_keys = noise(splits[1], (N_SECTION, N_MIRROR, SEQUENCE_LENGTH, KEY_VALUE_HEADS * HEAD_SIZE), 1.0, 6.0, ((0, 4), (1, 2), (2, 16)))
    saved_values = noise(splits[2], (N_SECTION, N_MIRROR, SEQUENCE_LENGTH, KEY_VALUE_HEADS * HEAD_SIZE), 1.0, 6.0, ((0, 4), (1, 2), (2, 16)))
    output_gradient = noise(splits[3], (N_SECTION, N_MIRROR, SEQUENCE_LENGTH, QUERY_HEADS * HEAD_SIZE), 16.0, 96.0, ((0, 4), (1, 2), (2, 16)))
    layer_input = noise(splits[4], (N_SECTION, N_MIRROR, SEQUENCE_LENGTH, D), 0.0625, 0.375, ((0, 4), (1, 2), (2, 16)))
    hadamard_signs = draw_hadamard_signs(jax.random.fold_in(splits[6], 71), 0)
    return {"queries": queries, "saved_keys": saved_keys, "saved_values": saved_values, "output_gradient": output_gradient, "layer_input": layer_input, "hadamard_signs": hadamard_signs}


score_scale = 144.0 ** (-0.5)
softcap = 50.0

def hadamard(order_size):
    positions = jnp.arange(order_size, dtype=jnp.int32)
    parity = jnp.zeros((order_size, order_size), jnp.int32)
    for bit_level in range(order_size.bit_length() - 1):
        digit_row = positions // 2 ** bit_level % 2
        parity = parity + digit_row[:, None] * digit_row[None, :]
    return (1 - 2 * (parity % 2)).astype(jnp.float32)

def rounded(operand):
    return lax.optimization_barrier(operand.astype(jnp.bfloat16)).astype(jnp.float32)

def group_grads(queries, saved_keys, saved_values, output_gradient, first_key):
    row_number = queries.shape[0]
    key_number = saved_keys.shape[0]
    window_rows = key_number - row_number
    query_place = jnp.arange(row_number, dtype=jnp.int32)[:, None]
    key_place = jnp.arange(key_number, dtype=jnp.int32)[None, :]
    distance = query_place + window_rows - key_place
    allowed = (distance >= 0) & (distance < window_rows) & (key_place >= first_key)
    query_wide = queries.astype(jnp.float32)
    key_wide = saved_keys.astype(jnp.float32)
    value_wide = saved_values.astype(jnp.float32)
    grad_wide = output_gradient.astype(jnp.float32)
    raw_score = jnp.einsum('rgd,ld->grl', query_wide, key_wide) * score_scale
    capped = jnp.tanh(raw_score / softcap)
    weights = jnp.where(allowed[None], jnp.exp(softcap * capped), 0.0)
    probability = weights / lax.optimization_barrier(jnp.sum(weights, axis=2, keepdims=True))
    prob_low = rounded(probability)
    attended = jnp.einsum('grl,ld->rgd', prob_low, value_wide)
    row_delta = lax.optimization_barrier(jnp.sum(grad_wide * attended, axis=2))
    prob_grad = jnp.einsum('rgd,ld->grl', grad_wide, value_wide)
    score_grad = probability * (prob_grad - jnp.transpose(row_delta)[:, :, None]) * (1.0 - capped * capped) * score_scale
    score_low = rounded(score_grad)
    query_gradient = jnp.einsum('grl,ld->rgd', score_low, key_wide)
    key_gradient = jnp.einsum('grl,rgd->ld', score_low, query_wide)
    value_gradient = jnp.einsum('grl,rgd->ld', prob_low, grad_wide)
    return (query_gradient, key_gradient, value_gradient)

def layer_grads(queries, saved_keys, saved_values, output_gradient, first_key):
    row_number = queries.shape[0]
    key_number = saved_keys.shape[0]
    query_heads = queries.reshape(row_number, KEY_VALUE_HEADS, QUERY_HEADS // KEY_VALUE_HEADS, HEAD_SIZE).transpose(1, 0, 2, 3)
    gradient_heads = output_gradient.reshape(row_number, KEY_VALUE_HEADS, QUERY_HEADS // KEY_VALUE_HEADS, HEAD_SIZE).transpose(1, 0, 2, 3)
    key_heads = saved_keys.reshape(key_number, KEY_VALUE_HEADS, HEAD_SIZE).transpose(1, 0, 2)
    value_heads = saved_values.reshape(key_number, KEY_VALUE_HEADS, HEAD_SIZE).transpose(1, 0, 2)

    def one_group(members):
        return group_grads(members[0], members[1], members[2], members[3], first_key)
    query_gradient, key_gradient, value_gradient = lax.map(one_group, (query_heads, key_heads, value_heads, gradient_heads))
    return (query_gradient.transpose(1, 0, 2, 3).reshape(row_number, QUERY_HEADS * HEAD_SIZE), key_gradient.transpose(1, 0, 2).reshape(key_number, KEY_VALUE_HEADS * HEAD_SIZE), value_gradient.transpose(1, 0, 2).reshape(key_number, KEY_VALUE_HEADS * HEAD_SIZE))

def sequence_grads(queries, saved_keys, saved_values, output_gradient):
    seq_rows = queries.shape[0]
    blocks_total = seq_rows // ROWS
    key_value_width = saved_keys.shape[1]
    front = jnp.zeros((WINDOW, key_value_width), saved_keys.dtype)
    padded_keys = jnp.concatenate([front, saved_keys], axis=0)
    padded_values = jnp.concatenate([front, saved_values], axis=0)

    def advance(totals, block_index):
        begin_row = block_index * ROWS
        q_block = lax.dynamic_slice_in_dim(queries, begin_row, ROWS, 0)
        g_block = lax.dynamic_slice_in_dim(output_gradient, begin_row, ROWS, 0)
        k_block = lax.dynamic_slice_in_dim(padded_keys, begin_row, WINDOW + ROWS, 0)
        v_block = lax.dynamic_slice_in_dim(padded_values, begin_row, WINDOW + ROWS, 0)
        query_gradient, key_gradient, value_gradient = layer_grads(q_block, k_block, v_block, g_block, WINDOW - begin_row)
        key_total = lax.dynamic_update_slice_in_dim(totals[0], lax.dynamic_slice_in_dim(totals[0], begin_row, WINDOW + ROWS, 0) + key_gradient, begin_row, 0)
        value_total = lax.dynamic_update_slice_in_dim(totals[1], lax.dynamic_slice_in_dim(totals[1], begin_row, WINDOW + ROWS, 0) + value_gradient, begin_row, 0)
        return ((key_total, value_total), query_gradient.astype(jnp.bfloat16))
    empty = jnp.zeros((WINDOW + seq_rows, key_value_width), jnp.float32)
    totals, query_blocks = lax.scan(advance, (empty, empty), jnp.arange(blocks_total, dtype=jnp.int32))
    query_gradient = query_blocks.reshape(seq_rows, QUERY_HEADS * HEAD_SIZE)
    return (query_gradient, totals[0][WINDOW:].astype(jnp.bfloat16), totals[1][WINDOW:].astype(jnp.bfloat16))

def rotate(partial_value, sign_row):
    key_value_width = partial_value.shape[1]
    outer_size = 2 ** ((key_value_width.bit_length() - 1) // 2)
    inner_size = key_value_width // outer_size
    signed = (partial_value * sign_row.astype(jnp.float32)[None, :]).reshape(partial_value.shape[0], outer_size, inner_size)
    inner_turn = jnp.einsum('dab,bc->dac', signed, hadamard(inner_size), precision=lax.Precision.HIGHEST)
    outer_turn = jnp.einsum('dac,ae->dec', inner_turn, hadamard(outer_size), precision=lax.Precision.HIGHEST)
    return outer_turn.reshape(partial_value.shape[0], key_value_width) * (1.0 / math.sqrt(key_value_width))

def rotated_sum(layer_input, value_gradient, sign_row):
    blocks_total = layer_input.shape[0] // ROWS

    def advance(total, block_index):
        begin_row = block_index * ROWS
        x_block = lax.dynamic_slice_in_dim(layer_input, begin_row, ROWS, 0)
        v_block = lax.dynamic_slice_in_dim(value_gradient, begin_row, ROWS, 0)
        partial_value = jnp.dot(x_block.T, v_block, preferred_element_type=jnp.float32)
        turned = rotate(partial_value, sign_row)
        return (total + rounded(turned), None)
    start_total = jnp.zeros((layer_input.shape[1], value_gradient.shape[1]), jnp.float32)
    total, unused = lax.scan(advance, start_total, jnp.arange(blocks_total, dtype=jnp.int32))
    return total

def reference(queries, saved_keys, saved_values, output_gradient, layer_input, hadamard_signs):
    key_value_width = KEY_VALUE_HEADS * HEAD_SIZE
    query_rows, key_list, value_list = ([], [], [])
    per_layer = [jnp.zeros((D, key_value_width), jnp.float32) for position in range(N_SECTION)]
    for position in range(N_SECTION):
        query_pair, key_pair, value_pair = ([], [], [])
        for mirror in range(N_MIRROR):
            layer_index = position if mirror == 0 else N_SECTION - 1 - position
            query_gradient, key_gradient, value_gradient = sequence_grads(queries[position, mirror], saved_keys[position, mirror], saved_values[position, mirror], output_gradient[position, mirror])
            per_layer[layer_index] = per_layer[layer_index] + rotated_sum(layer_input[position, mirror], value_gradient, hadamard_signs[layer_index])
            query_pair.append(query_gradient)
            key_pair.append(key_gradient)
            value_pair.append(value_gradient)
        query_rows.append(jnp.stack(query_pair))
        key_list.append(jnp.stack(key_pair))
        value_list.append(jnp.stack(value_pair))
    return (jnp.stack(query_rows), jnp.stack(key_list), jnp.stack(value_list), jnp.stack(per_layer))
```

```python
import math

import jax
import jax.numpy as jnp
import numpy as np
from jax import lax
from jax.experimental import pallas as pl
from jax.experimental.pallas import tpu as pltpu
from jax.sharding import PartitionSpec as P

KEY_VALUE_HEADS = 8
HEAD_SIZE = 128
WINDOW = 2048
SCORE_SCALE = 144.0 ** (-0.5)
SOFTCAP = 50.0
LOG2E = math.log2(math.e)


def dot(a, b, contract):
    return lax.dot_general(
        a, b, ((contract[:1], contract[1:]), ((), ())), preferred_element_type=jnp.float32
    )


def attention_kernel(
    parity_ref,
    own_ref,
    other_ref,
    dq_ref,
    own_kv_ref,
    other_kv_ref,
    k_s,
    v_s,
    kt_s,
    dk_s,
    dv_s,
    e_s,
    u_s,
    dp_s,
    l_s,
    d_s,
    dqt_s,
):
    chips, rows, _ = own_ref.shape
    span = WINDOW // rows
    head = HEAD_SIZE
    parity = parity_ref[0]
    step = pl.program_id(0)
    block = 2 * step + parity

    @pl.when(step == 0)
    def _():
        @pl.loop(0, chips)
        def _(j):
            mine, theirs = 2 * j + parity, 2 * j + 1 - parity
            for place, k, v in (
                (mine, own_ref[j, :, 4 * head : 5 * head], own_ref[j, :, 5 * head : 6 * head]),
                (theirs, other_ref[j, :, :head], other_ref[j, :, head:]),
            ):
                k_s[place] = k
                v_s[place] = v
                kt_s[place] = jnp.transpose(k)
                dk_s[place] = jnp.zeros((rows, head), jnp.float32)
                dv_s[place] = jnp.zeros((rows, head), jnp.float32)

    q2 = jnp.concatenate([own_ref[step, :, :head], own_ref[step, :, head : 2 * head]], axis=0)
    g2 = jnp.concatenate(
        [own_ref[step, :, 2 * head : 3 * head], own_ref[step, :, 3 * head : 4 * head]], axis=0
    )
    l_s[...] = jnp.zeros_like(l_s)
    d_s[...] = jnp.zeros_like(d_s)
    dqt_s[...] = jnp.zeros_like(dqt_s)

    def first_pass(place, mask):
        slot = place - block + span
        s = dot(k_s[place], q2, (1, 1))
        dp = dot(v_s[place], g2, (1, 1))
        capped = jnp.tanh(s * (SCORE_SCALE / SOFTCAP))
        e = jnp.exp2(capped * (SOFTCAP * LOG2E))
        if mask is not None:
            e = jnp.where(mask, e, 0.0)
        u = e - e * (capped * capped)
        l_s[...] += jnp.sum(e.reshape(rows // 8, 8, 2 * rows), axis=0)
        d_s[...] += jnp.sum((e * dp).reshape(rows // 8, 8, 2 * rows), axis=0)
        e_s[slot] = e.astype(jnp.bfloat16)
        u_s[slot] = u.astype(jnp.bfloat16)
        dp_s[slot] = dp

    key_place = lax.broadcasted_iota(jnp.int32, (rows, 2 * rows), 0)
    query_place = lax.broadcasted_iota(jnp.int32, (rows, 2 * rows), 1) % rows
    low = jnp.maximum(block - span + 1, 0)

    @pl.loop(low, block)
    def _(place):
        first_pass(place, None)

    first_pass(block, key_place <= query_place)

    @pl.when(block >= span)
    def _():
        first_pass(block - span, key_place > query_place)

    inverse = 1.0 / jnp.sum(l_s[...], axis=0, keepdims=True)
    delta = jnp.sum(d_s[...], axis=0, keepdims=True) * inverse
    inverse_t = jnp.transpose(jnp.broadcast_to(inverse, (head, 2 * rows)))
    g2_scaled = (g2.astype(jnp.float32) * inverse_t).astype(jnp.bfloat16)
    q2_scaled = (q2.astype(jnp.float32) * (inverse_t * SCORE_SCALE)).astype(jnp.bfloat16)

    @pl.loop(jnp.maximum(block - span, 0), block + 1)
    def _(place):
        slot = place - block + span
        score_grad = u_s[slot] * (dp_s[slot] - delta).astype(jnp.bfloat16)
        dv_s[place] += dot(e_s[slot], g2_scaled, (1, 0))
        dk_s[place] += dot(score_grad, q2_scaled, (1, 0))
        dqt_s[...] += dot(kt_s[place], score_grad, (1, 0))

    dq = jnp.transpose(dqt_s[...] * (inverse * SCORE_SCALE)).astype(jnp.bfloat16)
    dq_ref[0, :, :head] = dq[:rows]
    dq_ref[0, :, head:] = dq[rows:]

    @pl.when(step == chips - 1)
    def _():
        @pl.loop(0, chips)
        def _(j):
            mine, theirs = 2 * j + parity, 2 * j + 1 - parity
            for out_ref, place in ((own_kv_ref, mine), (other_kv_ref, theirs)):
                out_ref[j, :, :head] = dk_s[place].astype(jnp.bfloat16)
                out_ref[j, :, head:] = dv_s[place].astype(jnp.bfloat16)


def attention(parity, own, other):
    chips, rows, _ = own.shape
    head = HEAD_SIZE
    blocks = 2 * chips
    slots = WINDOW // rows + 1
    whole = pl.BlockSpec(memory_space=pltpu.VMEM)
    kv = jax.ShapeDtypeStruct((chips, rows, 2 * head), jnp.bfloat16)
    return pl.pallas_call(
        attention_kernel,
        grid=(chips,),
        out_shape=(kv, kv, kv),
        in_specs=[pl.BlockSpec(memory_space=pltpu.SMEM), whole, whole],
        out_specs=(
            pl.BlockSpec((1, rows, 2 * head), lambda t: (t, 0, 0)),
            whole,
            whole,
        ),
        scratch_shapes=[
            pltpu.VMEM((blocks, rows, head), jnp.bfloat16),
            pltpu.VMEM((blocks, rows, head), jnp.bfloat16),
            pltpu.VMEM((blocks, head, rows), jnp.bfloat16),
            pltpu.VMEM((blocks, rows, head), jnp.float32),
            pltpu.VMEM((blocks, rows, head), jnp.float32),
            pltpu.VMEM((slots, rows, 2 * rows), jnp.bfloat16),
            pltpu.VMEM((slots, rows, 2 * rows), jnp.bfloat16),
            pltpu.VMEM((slots, rows, 2 * rows), jnp.float32),
            pltpu.VMEM((8, 2 * rows), jnp.float32),
            pltpu.VMEM((8, 2 * rows), jnp.float32),
            pltpu.VMEM((head, 2 * rows), jnp.float32),
        ],
        compiler_params=pltpu.CompilerParams(
            dimension_semantics=("arbitrary",), vmem_limit_bytes=48 * 2**20
        ),
        cost_estimate=pl.CostEstimate(
            flops=10 * 112 * rows * rows * head,
            bytes_accessed=10 * 2**20,
            transcendentals=2 * 112 * rows * rows,
        ),
        name="attention",
    )(parity, own, other)


def hadamard(order_size):
    place = np.arange(order_size)
    both = place[:, None] & place[None, :]
    parity = np.zeros_like(both)
    for bit in range(order_size.bit_length() - 1):
        parity ^= both >> bit & 1
    return (1 - 2 * parity) / math.sqrt(order_size)


def body(queries, saved_keys, saved_values, output_gradient, layer_input, hadamard_signs):
    rows, width = saved_keys.shape[2:]
    depth = layer_input.shape[3]
    head = HEAD_SIZE
    heads = KEY_VALUE_HEADS
    ctx_count = lax.axis_size("ctx")
    sections = lax.axis_size("section")
    chips = ctx_count // 2
    lines = chips // 2
    ctx = lax.axis_index("ctx")
    section = lax.axis_index("section")
    mirror = lax.axis_index("mirror")
    core = ctx % 2
    line = ctx // 2 % lines
    far = ctx // (2 * lines)
    same_core = [[2 * chip + c for chip in range(chips)] for c in range(2)]

    def by_head(array):
        return array[0, 0].reshape(rows, heads, -1).transpose(1, 0, 2)

    def across(block):
        return lax.all_to_all(
            block, "ctx", 0, 0, tiled=True, axis_index_groups=same_core
        )

    def swap(block, axis, bit):
        route = [(i, i ^ bit) for i in range(lax.axis_size(axis))]
        return lax.ppermute(block, axis, route)

    sent = jnp.concatenate(
        [by_head(queries), by_head(output_gradient), by_head(saved_keys), by_head(saved_values)],
        axis=2,
    )
    own = across(sent)
    other = swap(own[:, :, 4 * head :], "ctx", 1)
    own, input_rows = lax.optimization_barrier((own, layer_input[0, 0]))

    chunks = input_rows.reshape(rows, 2, lines, depth // (2 * lines)).transpose(2, 0, 1, 3)
    chunks = chunks.reshape(lines, rows, depth // lines)
    columns = [lax.dynamic_index_in_dim(chunks, line, 0, keepdims=False)]
    for distance in range(1, lines):
        piece = lax.dynamic_index_in_dim(chunks, line ^ distance, 0, keepdims=False)
        columns.append(swap(piece, "ctx", 2 * distance))

    dq, own_kv, other_kv = attention(core.astype(jnp.int32).reshape(1), own, other)
    kv = own_kv.astype(jnp.float32) + swap(other_kv, "ctx", 1).astype(jnp.float32)
    kv = kv.astype(jnp.bfloat16)

    value_rows = kv[:, :, head:].reshape(2, 1, lines, rows, head).transpose(0, 1, 3, 2, 4)
    value_rows = jnp.broadcast_to(
        value_rows.reshape(2, 1, rows, lines * head), (2, lines, rows, lines * head)
    ).reshape(chips, rows, lines * head)
    back = across(jnp.concatenate([dq, kv[:, :, :head], value_rows], axis=2))
    query_gradient = back[:, :, : 2 * head].transpose(1, 0, 2).reshape(rows, heads * 2 * head)
    key_gradient = back[:, :, 2 * head : 3 * head].transpose(1, 0, 2).reshape(rows, width)
    values = back[:, :, 3 * head :].reshape(heads, rows, lines, head).transpose(2, 1, 0, 3)
    values = values.reshape(lines, rows, width)
    value_gradient = lax.dynamic_index_in_dim(values, line, 0, keepdims=False)

    total = None
    for distance in range(lines):
        part = dot(
            columns[distance],
            lax.dynamic_index_in_dim(values, line ^ distance, 0, keepdims=False),
            (0, 0),
        )
        total = part if total is None else total + part

    def halve(array, place, axis, bit):
        array = array.astype(jnp.bfloat16)
        keep = lax.dynamic_index_in_dim(array, place, 0, keepdims=False)
        give = lax.dynamic_index_in_dim(array, 1 - place, 0, keepdims=False)
        return keep.astype(jnp.float32) + swap(give, axis, bit).astype(jnp.float32)

    share = depth // (2 * ctx_count)
    total = total.reshape(2, 2, 2 * share * width).transpose(1, 0, 2).reshape(2, 2, 2 * share, width)
    total = halve(total, core, "ctx", 1)
    total = halve(total, far, "ctx", 2 * lines)
    total = total.reshape(2, share, width).astype(jnp.bfloat16)

    def routed(block, route):
        pairs = [(s * 2 + m, t * 2 + n) for (s, m), (t, n) in route]
        return lax.ppermute(block, ("section", "mirror"), pairs)

    places = range(sections)
    from_far = routed(total[0], [((s, 1), (sections - 1 - s, 0)) for s in places])
    from_far_second = routed(total[1], [((s, 1), (sections - 1 - s, 1)) for s in places])
    from_near = routed(total[1], [((s, 0), (s, 1)) for s in places])
    first = total[0].astype(jnp.float32) + from_far.astype(jnp.float32)
    second = from_near.astype(jnp.float32) + from_far_second.astype(jnp.float32)
    result = jnp.where(mirror == 0, first, second)

    signs = lax.dynamic_index_in_dim(hadamard_signs, section, 0, keepdims=False)
    turn = jnp.asarray(hadamard(width), jnp.bfloat16) * signs.astype(jnp.bfloat16)[:, None]
    rotated = dot(result.astype(jnp.bfloat16), turn, (1, 0))
    return (
        query_gradient[None, None],
        key_gradient[None, None],
        value_gradient[None, None],
        rotated[None],
    )


def solution(mesh):
    split = P("section", "mirror", "ctx", None)
    return jax.shard_map(
        body,
        mesh=mesh,
        in_specs=(split, split, split, split, split, P()),
        out_specs=(split, split, split, P("section", ("ctx", "mirror"), None)),
        check_vma=False,
    )
```

```python
import math

import jax
import jax.numpy as jnp
import numpy as np
from jax import lax
from jax.experimental import pallas as pl
from jax.experimental.pallas import tpu as pltpu
from jax.sharding import PartitionSpec as P

KEY_VALUE_HEADS = 8
HEAD_SIZE = 128
WINDOW = 2048
SCORE_SCALE = 144.0 ** (-0.5)
SOFTCAP = 50.0
LOG2E = math.log2(math.e)
WHOLE = pl.BlockSpec(memory_space=pltpu.VMEM)
SCALAR = pl.BlockSpec(memory_space=pltpu.SMEM)


def dot(a, b, contract):
    return lax.dot_general(
        a, b, ((contract[:1], contract[1:]), ((), ())), preferred_element_type=jnp.float32
    )


def pair(ref, first):
    at = first * HEAD_SIZE
    return jnp.concatenate(
        [ref[0, :, at : at + HEAD_SIZE], ref[0, :, at + HEAD_SIZE : at + 2 * HEAD_SIZE]],
        axis=0,
    )


def for_window(step, parity, span, one):
    block = 2 * step + parity
    for early in range(span // 2):
        @pl.when(step == early)
        def _():
            one(jnp.maximum(block - 2 * early - 1, 0), ["maybe"])
            one(block - 2 * early, ["middle"] * (2 * early) + ["near"])

    @pl.when(step >= span // 2)
    def _():
        one(block - span, ["far"] + ["middle"] * (span - 1) + ["near"])


def weights(s, kind, parity):
    rows = s.shape[0]
    capped = jnp.tanh(s * (SCORE_SCALE / SOFTCAP))
    e = jnp.exp2(capped * (SOFTCAP * LOG2E))
    if kind == "maybe":
        e = jnp.where(parity == 1, e, 0.0)
    elif kind != "middle":
        key_place = lax.broadcasted_iota(jnp.int32, s.shape, 0)
        query_place = lax.broadcasted_iota(jnp.int32, s.shape, 1) % rows
        allowed = key_place <= query_place if kind == "near" else key_place > query_place
        e = jnp.where(allowed, e, 0.0)
    return capped, e


def first_slot(place, kinds, block, span):
    return 0 if kinds == ["maybe"] else place - block + span


def blocks_at(ref, place, kinds):
    block = ref[pl.ds(place, len(kinds))]
    return block.reshape(len(kinds) * block.shape[1], block.shape[2])


def column_sums(x):
    return jnp.sum(x.reshape(x.shape[0] // 8, 8, x.shape[1]), axis=0)


def value_kernel(
    parity_ref, own_ref, own_kv_ref, other_ref, mine_ref, theirs_ref, k_s, dv_s, e_s, l_s
):
    chips, rows, _ = own_kv_ref.shape
    span = WINDOW // rows
    head = HEAD_SIZE
    parity = parity_ref[0]
    step = pl.program_id(0)
    block = 2 * step + parity

    @pl.when(step == 0)
    def _():
        @pl.loop(0, chips)
        def _(j):
            k_s[2 * j + parity] = own_kv_ref[j, :, :head]
            k_s[2 * j + 1 - parity] = other_ref[j, :, :head]
        dv_s[...] = jnp.zeros_like(dv_s)

    q2 = pair(own_ref, 0)
    g2 = pair(own_ref, 2)
    l_s[...] = jnp.zeros_like(l_s)

    def first_pass(place, kinds):
        slot = first_slot(place, kinds, block, span)
        sums = l_s[...]
        s = dot(blocks_at(k_s, place, kinds), q2, (1, 1))
        for i, kind in enumerate(kinds):
            _, e = weights(s[i * rows : (i + 1) * rows], kind, parity)
            sums = sums + column_sums(e)
            e_s[slot + i] = e.astype(jnp.bfloat16)
        l_s[...] = sums

    for_window(step, parity, span, first_pass)
    inverse = 1.0 / jnp.sum(l_s[...], axis=0, keepdims=True)
    inverse_t = jnp.transpose(jnp.broadcast_to(inverse, (head, 2 * rows)))
    g2_scaled = (g2.astype(jnp.float32) * inverse_t).astype(jnp.bfloat16)

    def second_pass(place, kinds):
        slot = first_slot(place, kinds, block, span)
        term = dot(blocks_at(e_s, slot, kinds), g2_scaled, (1, 0))
        dv_s[pl.ds(place, len(kinds))] += term.reshape(len(kinds), rows, head)

    for_window(step, parity, span, second_pass)

    @pl.when(step == chips - 1)
    def _():
        @pl.loop(0, chips)
        def _(j):
            mine_ref[j] = dv_s[2 * j + parity].astype(jnp.bfloat16)
            theirs_ref[j] = dv_s[2 * j + 1 - parity].astype(jnp.bfloat16)


def score_kernel(
    parity_ref,
    own_ref,
    own_kv_ref,
    other_ref,
    dq_ref,
    mine_ref,
    theirs_ref,
    k_s,
    v_s,
    kt_s,
    dk_s,
    u_s,
    dp_s,
    l_s,
    d_s,
    dqt_s,
):
    chips, rows, _ = own_kv_ref.shape
    span = WINDOW // rows
    head = HEAD_SIZE
    parity = parity_ref[0]
    step = pl.program_id(0)
    block = 2 * step + parity

    @pl.when(step == 0)
    def _():
        @pl.loop(0, chips)
        def _(j):
            mine, theirs = 2 * j + parity, 2 * j + 1 - parity
            for place, k, v in (
                (mine, own_kv_ref[j, :, :head], own_kv_ref[j, :, head:]),
                (theirs, other_ref[j, :, :head], other_ref[j, :, head:]),
            ):
                k_s[place] = k
                v_s[place] = v
                kt_s[place] = jnp.transpose(k)
        dk_s[...] = jnp.zeros_like(dk_s)

    q2 = pair(own_ref, 0)
    g2 = pair(own_ref, 2)
    l_s[...] = jnp.zeros_like(l_s)
    d_s[...] = jnp.zeros_like(d_s)
    dqt_s[...] = jnp.zeros_like(dqt_s)

    def first_pass(place, kinds):
        slot = first_slot(place, kinds, block, span)
        sums, products = l_s[...], d_s[...]
        s = dot(blocks_at(k_s, place, kinds), q2, (1, 1))
        dps = dot(blocks_at(v_s, place, kinds), g2, (1, 1))
        for i, kind in enumerate(kinds):
            capped, e = weights(s[i * rows : (i + 1) * rows], kind, parity)
            dp = dps[i * rows : (i + 1) * rows]
            sums = sums + column_sums(e)
            products = products + column_sums(e * dp)
            u_s[slot + i] = (e - e * (capped * capped)).astype(jnp.bfloat16)
            dp_s[slot + i] = dp
        l_s[...] = sums
        d_s[...] = products

    for_window(step, parity, span, first_pass)
    inverse = 1.0 / jnp.sum(l_s[...], axis=0, keepdims=True)
    delta = jnp.sum(d_s[...], axis=0, keepdims=True) * inverse
    inverse_t = jnp.transpose(jnp.broadcast_to(inverse * SCORE_SCALE, (head, 2 * rows)))
    q2_scaled = (q2.astype(jnp.float32) * inverse_t).astype(jnp.bfloat16)

    def second_pass(place, kinds):
        slot = first_slot(place, kinds, block, span)
        n = len(kinds)
        grads = [
            u_s[slot + i] * (dp_s[slot + i] - delta).astype(jnp.bfloat16) for i in range(n)
        ]
        score_grad = jnp.concatenate(grads, axis=0)
        dk_s[pl.ds(place, n)] += dot(score_grad, q2_scaled, (1, 0)).reshape(n, rows, head)
        turned = jnp.concatenate([kt_s[place + i] for i in range(n)], axis=1)
        dqt_s[...] += dot(turned, score_grad, (1, 0))

    for_window(step, parity, span, second_pass)
    dq = jnp.transpose(dqt_s[...] * (inverse * SCORE_SCALE)).astype(jnp.bfloat16)
    dq_ref[0, :, :head] = dq[:rows]
    dq_ref[0, :, head:] = dq[rows:]

    @pl.when(step == chips - 1)
    def _():
        @pl.loop(0, chips)
        def _(j):
            mine_ref[j] = dk_s[2 * j + parity].astype(jnp.bfloat16)
            theirs_ref[j] = dk_s[2 * j + 1 - parity].astype(jnp.bfloat16)


def attention_call(kernel, name, parity, own, other, with_query, scratch, products, vmem):
    chips, rows, _ = own.shape
    head = HEAD_SIZE
    grads = jax.ShapeDtypeStruct((chips, rows, head), jnp.bfloat16)
    out_shape, out_specs = [grads, grads], [WHOLE, WHOLE]
    if with_query:
        out_shape.insert(0, jax.ShapeDtypeStruct((chips, rows, 3 * head), jnp.bfloat16))
        out_specs.insert(0, pl.BlockSpec((1, rows, 2 * head), lambda t: (t, 0, 0)))
    return pl.pallas_call(
        kernel,
        grid=(chips,),
        out_shape=out_shape,
        in_specs=[
            SCALAR,
            pl.BlockSpec((1, rows, 4 * head), lambda t: (t, 0, 0)),
            pl.BlockSpec((chips, rows, 2 * head), lambda t: (0, 0, 2), pipeline_mode=pl.Buffered(1)),
            WHOLE,
        ],
        out_specs=out_specs,
        scratch_shapes=[pltpu.VMEM(shape, kind) for shape, kind in scratch],
        compiler_params=pltpu.CompilerParams(
            dimension_semantics=("arbitrary",), vmem_limit_bytes=vmem * 2**20
        ),
        cost_estimate=pl.CostEstimate(
            flops=2 * products * 112 * rows * rows * head,
            bytes_accessed=8 * 2**20,
            transcendentals=2 * 112 * rows * rows,
        ),
        name=name,
    )(parity, own, own, other)


def value_gradients(parity, own, other):
    chips, rows, _ = own.shape
    slots = WINDOW // rows + 1
    return attention_call(
        value_kernel,
        "value_gradients",
        parity,
        own,
        other,
        False,
        [
            ((2 * chips, rows, HEAD_SIZE), jnp.bfloat16),
            ((2 * chips, rows, HEAD_SIZE), jnp.float32),
            ((slots, rows, 2 * rows), jnp.bfloat16),
            ((8, 2 * rows), jnp.float32),
        ],
        4,
        28,
    )


def score_gradients(parity, own, other):
    chips, rows, _ = own.shape
    slots = WINDOW // rows + 1
    return attention_call(
        score_kernel,
        "score_gradients",
        parity,
        own,
        other,
        True,
        [
            ((2 * chips, rows, HEAD_SIZE), jnp.bfloat16),
            ((2 * chips, rows, HEAD_SIZE), jnp.bfloat16),
            ((2 * chips, HEAD_SIZE, rows), jnp.bfloat16),
            ((2 * chips, rows, HEAD_SIZE), jnp.float32),
            ((slots, rows, 2 * rows), jnp.bfloat16),
            ((slots, rows, 2 * rows), jnp.float32),
            ((8, 2 * rows), jnp.float32),
            ((8, 2 * rows), jnp.float32),
            ((HEAD_SIZE, 2 * rows), jnp.float32),
        ],
        8,
        60,
    )


def small_call(
    kernel,
    name,
    out_shape,
    scratch,
    flops,
    *operands,
    grid=None,
    in_specs=None,
    out_specs=None,
    kind=jnp.bfloat16,
    vmem=16,
    aliases=None,
):
    kinds = [jax.ShapeDtypeStruct(shape, kind) for shape in out_shape]
    specs = {}
    if grid is not None:
        specs = {"grid": grid}
    moved = sum(x.size * x.dtype.itemsize for x in operands) + sum(2 * math.prod(s) for s in out_shape)
    return pl.pallas_call(
        kernel,
        out_shape=kinds,
        in_specs=in_specs if in_specs is not None else [WHOLE] * len(operands),
        out_specs=out_specs if out_specs is not None else [WHOLE] * len(kinds),
        scratch_shapes=scratch,
        compiler_params=pltpu.CompilerParams(vmem_limit_bytes=vmem * 2**20),
        cost_estimate=pl.CostEstimate(flops=flops, bytes_accessed=moved, transcendentals=0),
        name=name,
        input_output_aliases=aliases or {},
        **specs,
    )(*operands)


def pack_heads(queries, output_gradient, saved_keys, saved_values):
    heads = KEY_VALUE_HEADS

    def kernel(*refs):
        out_ref, at = refs[-1], 0
        for ref in refs[:-1]:
            wide = ref.shape[1] // heads
            for g in range(heads):
                out_ref[g, :, at : at + wide] = ref[:, g * wide : (g + 1) * wide]
            at += wide

    rows = queries.shape[0]
    arrays = (queries, output_gradient, saved_keys, saved_values)
    part = rows // 4
    total = sum(x.shape[1] for x in arrays) // heads
    (packed,) = small_call(
        kernel,
        "pack_heads",
        [(heads, rows, total)],
        [],
        0,
        *arrays,
        grid=(rows // part,),
        in_specs=[pl.BlockSpec((part, x.shape[1]), lambda r: (r, 0)) for x in arrays],
        out_specs=[pl.BlockSpec((heads, part, total), lambda r: (0, r, 0))],
        vmem=60,
    )
    return packed


def pack_scores(payload, mine, theirs):
    def kernel(_, mine_ref, theirs_ref, out_ref):
        out_ref[...] = add(mine_ref[...], theirs_ref[...])

    chips, rows, head = mine.shape
    part = chips // 2
    block = pl.BlockSpec((part, rows, head), lambda t: (t, 0, 0))
    (packed,) = small_call(
        kernel,
        "pack_scores",
        [payload.shape],
        [],
        0,
        payload,
        mine,
        theirs,
        grid=(chips // part,),
        in_specs=[pl.BlockSpec(memory_space=pl.ANY), block, block],
        out_specs=[pl.BlockSpec((part, rows, head), lambda t: (t, 0, 2))],
        vmem=60,
        aliases={0: 0},
    )
    return packed


def unpack_scores(back):
    def kernel(in_ref, dq_ref, dk_ref):
        for g in range(heads):
            dq_ref[:, g * 2 * head : (g + 1) * 2 * head] = in_ref[g, :, : 2 * head]
            dk_ref[:, g * head : (g + 1) * head] = in_ref[g, :, 2 * head :]

    heads, rows, width = back.shape
    head = HEAD_SIZE
    part = rows // 4
    widths = (2 * head * heads, head * heads)
    return small_call(
        kernel,
        "unpack_scores",
        [(rows, w) for w in widths],
        [],
        0,
        back,
        grid=(rows // part,),
        in_specs=[pl.BlockSpec((heads, part, width), lambda r: (0, r, 0))],
        out_specs=[pl.BlockSpec((part, w), lambda r: (r, 0)) for w in widths],
    )


def pack_values(mine, theirs):
    def kernel(mine_ref, theirs_ref, out_ref):
        for x in range(2):
            for y in range(2):
                total = add(mine_ref[x, 0, y], theirs_ref[x, 0, y])
                for to in range(4):
                    out_ref[to // 2, 0, to % 2, 2 * x + y] = total

    chips, rows, head = mine.shape
    split = (2, 2, 2, rows, head)
    (packed,) = small_call(
        kernel,
        "pack_values",
        [split[:3] + (4, rows, head)],
        [],
        0,
        mine.reshape(split),
        theirs.reshape(split),
        grid=(2,),
        in_specs=[pl.BlockSpec((2, 1, 2, rows, head), lambda p: (0, p, 0, 0, 0))] * 2,
        out_specs=[pl.BlockSpec((2, 1, 2, 4, rows, head), lambda p: (0, p, 0, 0, 0, 0))],
        vmem=60,
    )
    return packed.reshape(chips, 4, rows, head)


def turn_input(place, input_rows):
    rows, depth = input_rows.shape
    share = depth // 16
    wide = 2 * HEAD_SIZE

    def kernel(place_ref, in_ref, *refs):
        out_refs, turned_s = refs[:-1], refs[-1]
        for at in range(0, depth, wide):
            turned_s[at : at + wide] = jnp.transpose(in_ref[:, at : at + wide])
        for distance, out_ref in enumerate(out_refs):
            to = place_ref[0] ^ distance
            for high in range(2):
                for core in range(2):
                    index = ((to // 2 * 2 + high) * 2 + to % 2) * 2 + core
                    piece = turned_s[pl.ds(pl.multiple_of(index * share, 16), share)]
                    out_ref[high, core * share : (core + 1) * share] = piece

    return small_call(
        kernel,
        "turn_input",
        [(2, 2 * share, rows)] * 4,
        [pltpu.VMEM((depth, rows), jnp.bfloat16)],
        0,
        place,
        input_rows,
        in_specs=[SCALAR, WHOLE],
    )


def input_product(place, columns, back):
    members = len(columns)
    heads, _, rows, head = back.shape
    share = columns[0].shape[1] // 2

    def kernel(place_ref, *refs):
        column_refs, back_ref = refs[:members], refs[members]
        give_ref, keep_ref, value_ref = refs[members + 1 :]
        member, core, high = place_ref[0], place_ref[1], place_ref[2]
        v = [
            jnp.concatenate([back_ref[0, member ^ d], back_ref[1, member ^ d]], axis=1)
            for d in range(members)
        ]
        value_ref[...] = v[0]
        v = jnp.concatenate(v, axis=0)
        for at, which_high in enumerate((1 - high, high)):
            for out_ref, which_core in ((give_ref, 1 - core), (keep_ref, core)):
                part = pl.ds(pl.multiple_of(which_core * share, 16), share)
                x = jnp.concatenate([ref[which_high, part] for ref in column_refs], axis=1)
                out_ref[at] = dot(x, v, (1, 0)).astype(jnp.bfloat16)

    once = pl.Buffered(1)
    halves = pl.BlockSpec((2, share, 2 * head), lambda g: (0, 0, g))
    return small_call(
        kernel,
        "input_product",
        [(2, share, heads * head)] * 2 + [(rows, heads * head)],
        [],
        8 * share * members * rows * heads * head,
        place,
        *columns,
        back,
        grid=(heads // 2,),
        in_specs=[SCALAR]
        + [pl.BlockSpec((2, 2 * share, rows), lambda g: (0, 0, 0), pipeline_mode=once)] * members
        + [pl.BlockSpec((2, members, rows, head), lambda g: (g, 0, 0, 0))],
        out_specs=[halves, halves, pl.BlockSpec((rows, 2 * head), lambda g: (0, g))],
        vmem=60,
    )


def add32(a, b):
    return a.astype(jnp.float32) + b.astype(jnp.float32)


def add(a, b):
    return add32(a, b).astype(jnp.bfloat16)


def cut_pieces(place, keep, got):
    def kernel(place_ref, keep_ref, got_ref, cross_other_ref, cross_own_ref, stay_ref, second_ref):
        mirror = place_ref[3]
        cross_other_ref[...] = add(keep_ref[0, 1 - mirror], got_ref[0, 1 - mirror])
        cross_own_ref[...] = add(keep_ref[1, 1 - mirror], got_ref[1, 1 - mirror])
        stay_ref[...] = add(keep_ref[0, mirror], got_ref[0, mirror])
        second_ref[...] = add(keep_ref[1, 1], got_ref[1, 1])

    return small_call(
        kernel,
        "cut_pieces",
        [keep.shape[2:]] * 4,
        [],
        0,
        place,
        keep,
        got,
        in_specs=[SCALAR, WHOLE, WHOLE],
    )


def finish(place, signs, turn, pieces):
    def kernel(place_ref, signs_ref, turn_ref, own_ref, got_ref, near_ref, near2_ref, far_ref, other_ref, out_ref):
        own = add32(own_ref[...], got_ref[...])
        total = jnp.where(place_ref[3] == 0, own, far_ref[...].astype(jnp.float32))
        total = total + add32(near_ref[...], near2_ref[...]) + other_ref[...].astype(jnp.float32)
        signs = signs_ref[pl.ds(place_ref[4], 1)].astype(jnp.float32)
        out_ref[...] = dot((total * signs).astype(jnp.bfloat16), turn_ref[...], (1, 0))

    own = pieces[0]
    (out,) = small_call(
        kernel,
        "finish",
        [own.shape],
        [],
        2 * own.size * own.shape[1],
        place,
        signs,
        turn,
        *pieces,
        in_specs=[SCALAR] + [WHOLE] * 8,
        kind=jnp.float32,
    )
    return out


def hadamard(order_size):
    place = np.arange(order_size)
    both = place[:, None] & place[None, :]
    parity = np.zeros_like(both)
    for bit in range(order_size.bit_length() - 1):
        parity ^= both >> bit & 1
    return (1 - 2 * parity) / math.sqrt(order_size)


def body(queries, saved_keys, saved_values, output_gradient, layer_input, hadamard_signs):
    width = saved_keys.shape[3]
    head = HEAD_SIZE
    chips = lax.axis_size("ctx") // 2
    sections = lax.axis_size("section")
    ctx = lax.axis_index("ctx").astype(jnp.int32)
    section = lax.axis_index("section").astype(jnp.int32)
    mirror = lax.axis_index("mirror").astype(jnp.int32)
    core = ctx & 1
    same_core = [[2 * chip + c for chip in range(chips)] for c in range(2)]
    member = (ctx >> 3) * 2 + (ctx >> 1 & 1)
    place = jnp.stack([member, core, ctx >> 2 & 1, mirror, section])

    def across(block):
        return lax.all_to_all(block, "ctx", 0, 0, tiled=True, axis_index_groups=same_core)

    def swap(block, bits):
        return lax.ppermute(block, "ctx", [(i, i ^ bits) for i in range(2 * chips)])

    turned = turn_input(place, layer_input[0, 0])
    own = across(
        pack_heads(queries[0, 0], output_gradient[0, 0], saved_keys[0, 0], saved_values[0, 0])
    )
    own, *turned = lax.optimization_barrier((own, *turned))
    other = swap(own[:, :, 4 * head :], 1)
    parity = core.reshape(1)
    columns = turned[:1] + [swap(turned[d], (d & 1) * 2 + (d >> 1) * 8) for d in range(1, 4)]

    dv_mine, dv_theirs = value_gradients(parity, own, other)
    values = pack_values(dv_mine, swap(dv_theirs, 1))
    values, own, *columns = lax.optimization_barrier((values, own, *columns))
    values_back = across(values)

    scores, dk_mine, dk_theirs = score_gradients(parity, own, other)
    scores = pack_scores(scores, dk_mine, swap(dk_theirs, 1))
    values_back, scores = lax.optimization_barrier((values_back, scores))
    scores_back = across(scores)
    give, keep, value_gradient = input_product(place, columns, values_back)
    got = swap(give, 1)

    keep = keep.reshape(2, 2, -1, width)
    got = got.reshape(keep.shape)
    sections = lax.axis_size("section")
    cross_other, cross_own, stay_other, second_own = cut_pieces(place, keep, got)

    def routed(block, route, group):
        axes = ("section", "ctx", "mirror")
        pairs = [
            ((s * 2 * chips + i) * 2 + m, (t * 2 * chips + (i ^ group)) * 2 + n)
            for (s, m), (t, n) in route
            for i in range(2 * chips)
        ]
        return lax.ppermute(block, axes, pairs)

    far = [((s, 1), (sections - 1 - s, 1)) for s in range(sections)]
    cross = [((s, 1), (sections - 1 - s, 0)) for s in range(sections)]
    cross += [((s, 0), (s, 1)) for s in range(sections)]
    near_other = routed(cross_other, cross, 4)
    other = routed(stay_other, far + [((s, 0), (s, 0)) for s in range(sections)], 4)
    cross_own, second_own, scores_back = lax.optimization_barrier((cross_own, second_own, scores_back))
    near_own = routed(cross_own, cross, 0)
    far_own = routed(second_own, far, 0)
    rotated = finish(
        place,
        hadamard_signs,
        jnp.asarray(hadamard(width), jnp.bfloat16),
        (keep[1, 0], got[1, 0], near_other, near_own, far_own, other),
    )
    query_gradient, key_gradient = unpack_scores(scores_back)
    return (
        query_gradient[None, None],
        key_gradient[None, None],
        value_gradient[None, None],
        rotated[None],
    )


def solution(mesh):
    split = P("section", "mirror", "ctx", None)
    return jax.shard_map(
        body,
        mesh=mesh,
        in_specs=(split, split, split, split, split, P()),
        out_specs=(split, split, split, P("section", ("ctx", "mirror"), None)),
        check_vma=False,
    )
```

```python
import math

import jax
import jax.numpy as jnp
import numpy as np
from jax import lax
from jax.experimental import pallas as pl
from jax.experimental.pallas import tpu as pltpu
from jax.sharding import PartitionSpec as P

KEY_VALUE_HEADS = 8
HEAD_SIZE = 128
WINDOW = 2048
SCORE_SCALE = 144.0 ** (-0.5)
SOFTCAP = 50.0
LOG2E = math.log2(math.e)
WHOLE = pl.BlockSpec(memory_space=pltpu.VMEM)
SCALAR = pl.BlockSpec(memory_space=pltpu.SMEM)


def dot(a, b, contract):
    return lax.dot_general(
        a, b, ((contract[:1], contract[1:]), ((), ())), preferred_element_type=jnp.float32
    )


def pair(ref, first):
    at = first * HEAD_SIZE
    return jnp.concatenate(
        [ref[0, :, at : at + HEAD_SIZE], ref[0, :, at + HEAD_SIZE : at + 2 * HEAD_SIZE]],
        axis=0,
    )


def full_window(span):
    return ["far"] + ["middle"] * (span - 1) + ["near"]


def early_windows(step, parity, span, one):
    block = 2 * step + parity
    for early in range(span // 2):

        @pl.when(step == early)
        def _():
            distance = 2 * early
            one(
                [
                    (jnp.maximum(block - distance - 1, 0), 0, ["maybe"]),
                    (block - distance, 1, ["middle"] * distance + ["near"]),
                ]
            )


def weights(s, kind, parity):
    rows = s.shape[0]
    capped = jnp.tanh(s * (SCORE_SCALE / SOFTCAP))
    e = jnp.exp2(capped * (SOFTCAP * LOG2E))
    if kind == "maybe":
        e = jnp.where(parity == 1, e, 0.0)
    elif kind != "middle":
        key_place = lax.broadcasted_iota(jnp.int32, s.shape, 0)
        query_place = lax.broadcasted_iota(jnp.int32, s.shape, 1) % rows
        allowed = key_place <= query_place if kind == "near" else key_place > query_place
        e = jnp.where(allowed, e, 0.0)
    return capped, e


def blocks_at(ref, place, kinds):
    block = ref[pl.ds(place, len(kinds))]
    return block.reshape(len(kinds) * block.shape[1], block.shape[2])


def column_sums(x):
    return jnp.sum(x.reshape(x.shape[0] // 8, 8, x.shape[1]), axis=0)


def turned_rows(x, scale):
    scale = jnp.transpose(jnp.broadcast_to(scale, (x.shape[1], x.shape[0])))
    return (x.astype(jnp.float32) * scale).astype(jnp.bfloat16)


def store_query_gradient(ref, turned):
    rows = turned.shape[1] // 2
    dq = jnp.transpose(turned).astype(jnp.bfloat16)
    ref[0, :, : turned.shape[0]] = dq[:rows]
    ref[0, :, turned.shape[0] :] = dq[rows:]


def value_kernel(
    parity_ref,
    own_ref,
    own_kv_ref,
    other_ref,
    dq_ref,
    dk_ref,
    mine_ref,
    theirs_ref,
    k_s,
    v_s,
    kt_s,
    dv_s,
    e_s,
    u_s,
    dp_s,
):
    chips, rows, _ = own_kv_ref.shape
    span = WINDOW // rows
    head = HEAD_SIZE
    parity = parity_ref[0]
    step = pl.program_id(0)
    block = 2 * step + parity

    @pl.when(step == 0)
    def _():
        @pl.loop(0, chips)
        def _(j):
            k_s[2 * j + parity] = own_kv_ref[j, :, :head]
            k_s[2 * j + 1 - parity] = other_ref[j, :, :head]

        @pl.loop(0, span // 2)
        def _(j):
            v_s[2 * j + parity] = own_kv_ref[j, :, head:]
            v_s[2 * j + 1 - parity] = other_ref[j, :, head:]

        @pl.loop(0, span)
        def _(j):
            kt_s[j] = jnp.transpose(k_s[j])

        dv_s[...] = jnp.zeros_like(dv_s)
        dk_ref[...] = jnp.zeros_like(dk_ref)

    q2 = pair(own_ref, 0)
    g2 = pair(own_ref, 2)

    def early(runs):
        sums = jnp.zeros((8, 2 * rows), jnp.float32)
        products = jnp.zeros((8, 2 * rows), jnp.float32)
        for place, slot, kinds in runs:
            s = dot(blocks_at(k_s, place, kinds), q2, (1, 1))
            dps = dot(blocks_at(v_s, place, kinds), g2, (1, 1))
            for i, kind in enumerate(kinds):
                capped, e = weights(s[i * rows : (i + 1) * rows], kind, parity)
                dp = dps[i * rows : (i + 1) * rows]
                sums = sums + column_sums(e)
                products = products + column_sums(e * dp)
                e_s[slot + i] = e.astype(jnp.bfloat16)
                u_s[slot + i] = (e - e * (capped * capped)).astype(jnp.bfloat16)
                dp_s[slot + i] = dp
        inverse = 1.0 / jnp.sum(sums, axis=0, keepdims=True)
        delta = jnp.sum(products, axis=0, keepdims=True) * inverse
        g2_scaled = turned_rows(g2, inverse)
        q2_scaled = turned_rows(q2, inverse * SCORE_SCALE)
        turned = jnp.zeros((head, 2 * rows), jnp.float32)
        for place, slot, kinds in runs:
            n = len(kinds)
            grad = [
                u_s[slot + i] * (dp_s[slot + i] - delta).astype(jnp.bfloat16) for i in range(n)
            ]
            grad = jnp.concatenate(grad, axis=0)
            term = dot(blocks_at(e_s, slot, kinds), g2_scaled, (1, 0))
            dv_s[pl.ds(place, n)] += term.reshape(n, rows, head)
            dk_ref[pl.ds(place, n)] += dot(grad, q2_scaled, (1, 0)).reshape(n, rows, head)
            keys = jnp.concatenate([kt_s[place + i] for i in range(n)], axis=1)
            turned = turned + dot(keys, grad, (1, 0))
        store_query_gradient(dq_ref, turned * (inverse * SCORE_SCALE))

    early_windows(step, parity, span, early)

    @pl.when(step >= span // 2)
    def _():
        kinds = full_window(span)
        place = block - span
        s = dot(blocks_at(k_s, place, kinds), q2, (1, 1))
        sums = jnp.zeros((8, 2 * rows), jnp.float32)
        for i, kind in enumerate(kinds):
            _, e = weights(s[i * rows : (i + 1) * rows], kind, parity)
            sums = sums + column_sums(e)
            e_s[i] = e.astype(jnp.bfloat16)
        g2_scaled = turned_rows(g2, 1.0 / jnp.sum(sums, axis=0, keepdims=True))
        term = dot(blocks_at(e_s, 0, kinds), g2_scaled, (1, 0))
        dv_s[pl.ds(place, span + 1)] += term.reshape(span + 1, rows, head)

    @pl.when(step == chips - 1)
    def _():
        @pl.loop(0, chips)
        def _(j):
            mine_ref[j] = dv_s[2 * j + parity].astype(jnp.bfloat16)
            theirs_ref[j] = dv_s[2 * j + 1 - parity].astype(jnp.bfloat16)


def score_kernel(
    parity_ref,
    own_ref,
    own_kv_ref,
    other_ref,
    _,
    dk_ref,
    dq_ref,
    mine_ref,
    theirs_ref,
    k_s,
    v_s,
    kt_s,
    dk_s,
    u_s,
    dp_s,
):
    chips, rows, _ = own_kv_ref.shape
    span = WINDOW // rows
    head = HEAD_SIZE
    parity = parity_ref[0]
    step = pl.program_id(0)
    place = 2 * (step + span // 2) + parity - span

    @pl.when(step == 0)
    def _():
        @pl.loop(0, chips)
        def _(j):
            mine, theirs = 2 * j + parity, 2 * j + 1 - parity
            for to, k, v in (
                (mine, own_kv_ref[j, :, :head], own_kv_ref[j, :, head:]),
                (theirs, other_ref[j, :, :head], other_ref[j, :, head:]),
            ):
                k_s[to] = k
                v_s[to] = v
                kt_s[to] = jnp.transpose(k)

        dk_s[:span] = dk_ref[...]
        dk_s[span:] = jnp.zeros((2 * chips - span, rows, head), jnp.float32)

    q2 = pair(own_ref, 0)
    g2 = pair(own_ref, 2)
    kinds = full_window(span)
    s = dot(blocks_at(k_s, place, kinds), q2, (1, 1))
    dps = dot(blocks_at(v_s, place, kinds), g2, (1, 1))
    sums = jnp.zeros((8, 2 * rows), jnp.float32)
    products = jnp.zeros((8, 2 * rows), jnp.float32)
    for i, kind in enumerate(kinds):
        capped, e = weights(s[i * rows : (i + 1) * rows], kind, parity)
        dp = dps[i * rows : (i + 1) * rows]
        sums = sums + column_sums(e)
        products = products + column_sums(e * dp)
        u_s[i] = (e - e * (capped * capped)).astype(jnp.bfloat16)
        dp_s[i] = dp
    inverse = 1.0 / jnp.sum(sums, axis=0, keepdims=True)
    delta = jnp.sum(products, axis=0, keepdims=True) * inverse
    q2_scaled = turned_rows(q2, inverse * SCORE_SCALE)
    grad = [u_s[i] * (dp_s[i] - delta).astype(jnp.bfloat16) for i in range(span + 1)]
    grad = jnp.concatenate(grad, axis=0)
    dk_s[pl.ds(place, span + 1)] += dot(grad, q2_scaled, (1, 0)).reshape(span + 1, rows, head)
    keys = jnp.concatenate([kt_s[place + i] for i in range(span + 1)], axis=1)
    store_query_gradient(dq_ref, dot(keys, grad, (1, 0)) * (inverse * SCORE_SCALE))

    @pl.when(step == chips - span // 2 - 1)
    def _():
        @pl.loop(0, chips)
        def _(j):
            mine_ref[j] = dk_s[2 * j + parity].astype(jnp.bfloat16)
            theirs_ref[j] = dk_s[2 * j + 1 - parity].astype(jnp.bfloat16)


def attention_call(kernel, name, operands, first, more_in, more_out, scratch, products, vmem):
    chips, rows, _ = operands[1].shape
    head = HEAD_SIZE
    early = WINDOW // rows // 2
    grads = jax.ShapeDtypeStruct((chips, rows, head), jnp.bfloat16)
    payload = jax.ShapeDtypeStruct((chips, rows, 3 * head), jnp.bfloat16)

    def query_block(t):
        return (t + first if first else jnp.minimum(t, early - 1), 0, 0)

    return pl.pallas_call(
        kernel,
        grid=(chips - first,),
        out_shape=[payload] + [shape for shape, _ in more_out] + [grads, grads],
        in_specs=[
            SCALAR,
            pl.BlockSpec((1, rows, 4 * head), lambda t: (t + first, 0, 0)),
            pl.BlockSpec((chips, rows, 2 * head), lambda t: (0, 0, 2), pipeline_mode=pl.Buffered(1)),
            WHOLE,
        ]
        + more_in,
        out_specs=[pl.BlockSpec((1, rows, 2 * head), query_block)]
        + [spec for _, spec in more_out]
        + [WHOLE, WHOLE],
        scratch_shapes=[pltpu.VMEM(shape, kind) for shape, kind in scratch],
        input_output_aliases={4: 0} if first else {},
        compiler_params=pltpu.CompilerParams(
            dimension_semantics=("arbitrary",), vmem_limit_bytes=vmem * 2**20
        ),
        cost_estimate=pl.CostEstimate(
            flops=2 * products * 112 * rows * rows * head,
            bytes_accessed=8 * 2**20,
            transcendentals=2 * 112 * rows * rows,
        ),
        name=name,
    )(*operands)


def value_gradients(parity, own, other):
    chips, rows, _ = own.shape
    span = WINDOW // rows
    head = HEAD_SIZE
    dk = jax.ShapeDtypeStruct((span, rows, head), jnp.float32)
    return attention_call(
        value_kernel,
        "value_gradients",
        (parity, own, own, other),
        0,
        [],
        [(dk, WHOLE)],
        [
            ((2 * chips, rows, head), jnp.bfloat16),
            ((span, rows, head), jnp.bfloat16),
            ((span, head, rows), jnp.bfloat16),
            ((2 * chips, rows, head), jnp.float32),
            ((span + 1, rows, 2 * rows), jnp.bfloat16),
            ((span, rows, 2 * rows), jnp.bfloat16),
            ((span, rows, 2 * rows), jnp.float32),
        ],
        4,
        28,
    )


def score_gradients(parity, own, other, payload, dk):
    chips, rows, _ = own.shape
    span = WINDOW // rows
    head = HEAD_SIZE
    return attention_call(
        score_kernel,
        "score_gradients",
        (parity, own, own, other, payload, dk),
        span // 2,
        [pl.BlockSpec(memory_space=pl.ANY), WHOLE],
        [],
        [
            ((2 * chips, rows, head), jnp.bfloat16),
            ((2 * chips, rows, head), jnp.bfloat16),
            ((2 * chips, head, rows), jnp.bfloat16),
            ((2 * chips, rows, head), jnp.float32),
            ((span + 1, rows, 2 * rows), jnp.bfloat16),
            ((span + 1, rows, 2 * rows), jnp.float32),
        ],
        8,
        60,
    )


def small_call(
    kernel,
    name,
    out_shape,
    scratch,
    flops,
    *operands,
    grid=None,
    in_specs=None,
    out_specs=None,
    kind=jnp.bfloat16,
    vmem=16,
    aliases=None,
):
    kinds = [jax.ShapeDtypeStruct(shape, kind) for shape in out_shape]
    specs = {}
    if grid is not None:
        specs = {"grid": grid}
    moved = sum(x.size * x.dtype.itemsize for x in operands) + sum(2 * math.prod(s) for s in out_shape)
    return pl.pallas_call(
        kernel,
        out_shape=kinds,
        in_specs=in_specs if in_specs is not None else [WHOLE] * len(operands),
        out_specs=out_specs if out_specs is not None else [WHOLE] * len(kinds),
        scratch_shapes=scratch,
        compiler_params=pltpu.CompilerParams(vmem_limit_bytes=vmem * 2**20),
        cost_estimate=pl.CostEstimate(flops=flops, bytes_accessed=moved, transcendentals=0),
        name=name,
        input_output_aliases=aliases or {},
        **specs,
    )(*operands)


def pack_heads(queries, output_gradient, saved_keys, saved_values):
    heads = KEY_VALUE_HEADS

    def kernel(*refs):
        out_ref, at = refs[-1], 0
        for ref in refs[:-1]:
            wide = ref.shape[1] // heads
            for g in range(heads):
                out_ref[g, :, at : at + wide] = ref[:, g * wide : (g + 1) * wide]
            at += wide

    rows = queries.shape[0]
    arrays = (queries, output_gradient, saved_keys, saved_values)
    part = rows // 2
    total = sum(x.shape[1] for x in arrays) // heads
    (packed,) = small_call(
        kernel,
        "pack_heads",
        [(heads, rows, total)],
        [],
        0,
        *arrays,
        grid=(rows // part,),
        in_specs=[pl.BlockSpec((part, x.shape[1]), lambda r: (r, 0)) for x in arrays],
        out_specs=[pl.BlockSpec((heads, part, total), lambda r: (0, r, 0))],
        vmem=60,
    )
    return packed


def pack_scores(payload, mine, theirs):
    def kernel(_, mine_ref, theirs_ref, out_ref):
        out_ref[...] = add(mine_ref[...], theirs_ref[...])

    chips, rows, head = mine.shape
    part = chips // 2
    block = pl.BlockSpec((part, rows, head), lambda t: (t, 0, 0))
    (packed,) = small_call(
        kernel,
        "pack_scores",
        [payload.shape],
        [],
        0,
        payload,
        mine,
        theirs,
        grid=(chips // part,),
        in_specs=[pl.BlockSpec(memory_space=pl.ANY), block, block],
        out_specs=[pl.BlockSpec((part, rows, head), lambda t: (t, 0, 2))],
        vmem=60,
        aliases={0: 0},
    )
    return packed


def unpack_scores(back):
    def kernel(in_ref, dq_ref, dk_ref):
        for g in range(heads):
            dq_ref[:, g * 2 * head : (g + 1) * 2 * head] = in_ref[g, :, : 2 * head]
            dk_ref[:, g * head : (g + 1) * head] = in_ref[g, :, 2 * head :]

    heads, rows, width = back.shape
    head = HEAD_SIZE
    part = rows // 4
    widths = (2 * head * heads, head * heads)
    return small_call(
        kernel,
        "unpack_scores",
        [(rows, w) for w in widths],
        [],
        0,
        back,
        grid=(rows // part,),
        in_specs=[pl.BlockSpec((heads, part, width), lambda r: (0, r, 0))],
        out_specs=[pl.BlockSpec((part, w), lambda r: (r, 0)) for w in widths],
    )


def pack_values(mine, theirs):
    def kernel(mine_ref, theirs_ref, out_ref):
        for x in range(2):
            for y in range(2):
                total = add(mine_ref[x, 0, y], theirs_ref[x, 0, y])
                for to in range(4):
                    out_ref[to // 2, 0, to % 2, 2 * x + y] = total

    chips, rows, head = mine.shape
    split = (2, 2, 2, rows, head)
    (packed,) = small_call(
        kernel,
        "pack_values",
        [split[:3] + (4, rows, head)],
        [],
        0,
        mine.reshape(split),
        theirs.reshape(split),
        grid=(2,),
        in_specs=[pl.BlockSpec((2, 1, 2, rows, head), lambda p: (0, p, 0, 0, 0))] * 2,
        out_specs=[pl.BlockSpec((2, 1, 2, 4, rows, head), lambda p: (0, p, 0, 0, 0, 0))],
        vmem=16,
    )
    return packed.reshape(chips, 4, rows, head)


def turn_input(place, input_rows):
    rows, depth = input_rows.shape
    share = depth // 16
    wide = 2 * HEAD_SIZE

    def kernel(place_ref, in_ref, *refs):
        out_refs, turned_s = refs[:-1], refs[-1]
        for at in range(0, depth, wide):
            turned_s[at : at + wide] = jnp.transpose(in_ref[:, at : at + wide])
        for distance, out_ref in enumerate(out_refs):
            to = place_ref[0] ^ distance
            for high in range(2):
                for core in range(2):
                    index = ((to // 2 * 2 + high) * 2 + to % 2) * 2 + core
                    piece = turned_s[pl.ds(pl.multiple_of(index * share, 16), share)]
                    out_ref[high, core * share : (core + 1) * share] = piece

    return small_call(
        kernel,
        "turn_input",
        [(2, 2 * share, rows)] * 4,
        [pltpu.VMEM((depth, rows), jnp.bfloat16)],
        0,
        place,
        input_rows,
        in_specs=[SCALAR, WHOLE],
    )


def input_product(place, columns, back):
    members = len(columns)
    heads, _, rows, head = back.shape
    share = columns[0].shape[1] // 2

    def kernel(place_ref, *refs):
        column_refs, back_ref = refs[:members], refs[members]
        give_ref, keep_ref, value_ref = refs[members + 1 :]
        member, core, high = place_ref[0], place_ref[1], place_ref[2]
        v = [
            jnp.concatenate([back_ref[0, member ^ d], back_ref[1, member ^ d]], axis=1)
            for d in range(members)
        ]
        value_ref[...] = v[0]
        v = jnp.concatenate(v, axis=0)
        for at, which_high in enumerate((1 - high, high)):
            for out_ref, which_core in ((give_ref, 1 - core), (keep_ref, core)):
                part = pl.ds(pl.multiple_of(which_core * share, 16), share)
                x = jnp.concatenate([ref[which_high, part] for ref in column_refs], axis=1)
                out_ref[at] = dot(x, v, (1, 0)).astype(jnp.bfloat16)

    once = pl.Buffered(1)
    halves = pl.BlockSpec((2, share, 2 * head), lambda g: (0, 0, g))
    return small_call(
        kernel,
        "input_product",
        [(2, share, heads * head)] * 2 + [(rows, heads * head)],
        [],
        8 * share * members * rows * heads * head,
        place,
        *columns,
        back,
        grid=(heads // 2,),
        in_specs=[SCALAR]
        + [pl.BlockSpec((2, 2 * share, rows), lambda g: (0, 0, 0), pipeline_mode=once)] * members
        + [pl.BlockSpec((2, members, rows, head), lambda g: (g, 0, 0, 0))],
        out_specs=[halves, halves, pl.BlockSpec((rows, 2 * head), lambda g: (0, g))],
        vmem=60,
    )


def add32(a, b):
    return a.astype(jnp.float32) + b.astype(jnp.float32)


def add(a, b):
    return add32(a, b).astype(jnp.bfloat16)


def cut_pieces(place, keep, got):
    def kernel(place_ref, keep_ref, got_ref, cross_other_ref, cross_own_ref, stay_ref, second_ref, own_ref):
        mirror = place_ref[3]
        cross_other_ref[...] = add(keep_ref[0, 1 - mirror], got_ref[0, 1 - mirror])
        cross_own_ref[...] = add(keep_ref[1, 1 - mirror], got_ref[1, 1 - mirror])
        stay_ref[...] = add(keep_ref[0, mirror], got_ref[0, mirror])
        second_ref[...] = add(keep_ref[1, 1], got_ref[1, 1])
        own_ref[...] = add(keep_ref[1, 0], got_ref[1, 0])

    return small_call(
        kernel,
        "cut_pieces",
        [keep.shape[2:]] * 5,
        [],
        0,
        place,
        keep,
        got,
        in_specs=[SCALAR, WHOLE, WHOLE],
    )


def finish(place, signs, turn, pieces):
    def kernel(place_ref, signs_ref, turn_ref, own_ref, near_ref, near2_ref, far_ref, other_ref, out_ref):
        total = jnp.where(place_ref[3] == 0, own_ref[...], far_ref[...]).astype(jnp.float32)
        total = total + add32(near_ref[...], near2_ref[...]) + other_ref[...].astype(jnp.float32)
        signs = signs_ref[pl.ds(place_ref[4], 1)].astype(jnp.float32)
        out_ref[...] = dot((total * signs).astype(jnp.bfloat16), turn_ref[...], (1, 0))

    own = pieces[0]
    (out,) = small_call(
        kernel,
        "finish",
        [own.shape],
        [],
        2 * own.size * own.shape[1],
        place,
        signs,
        turn,
        *pieces,
        in_specs=[SCALAR] + [WHOLE] * 7,
        kind=jnp.float32,
    )
    return out


def hadamard(order_size):
    place = np.arange(order_size)
    both = place[:, None] & place[None, :]
    parity = np.zeros_like(both)
    for bit in range(order_size.bit_length() - 1):
        parity ^= both >> bit & 1
    return (1 - 2 * parity) / math.sqrt(order_size)


def body(queries, saved_keys, saved_values, output_gradient, layer_input, hadamard_signs):
    width = saved_keys.shape[3]
    head = HEAD_SIZE
    chips = lax.axis_size("ctx") // 2
    sections = lax.axis_size("section")
    ctx = lax.axis_index("ctx").astype(jnp.int32)
    section = lax.axis_index("section").astype(jnp.int32)
    mirror = lax.axis_index("mirror").astype(jnp.int32)
    core = ctx & 1
    same_core = [[2 * chip + c for chip in range(chips)] for c in range(2)]
    member = (ctx >> 3) * 2 + (ctx >> 1 & 1)
    place = jnp.stack([member, core, ctx >> 2 & 1, mirror, section])

    def across(block):
        return lax.all_to_all(block, "ctx", 0, 0, tiled=True, axis_index_groups=same_core)

    def swap(block, bits):
        return lax.ppermute(block, "ctx", [(i, i ^ bits) for i in range(2 * chips)])

    turned = turn_input(place, layer_input[0, 0])
    own = across(
        pack_heads(queries[0, 0], output_gradient[0, 0], saved_keys[0, 0], saved_values[0, 0])
    )
    own, *turned = lax.optimization_barrier((own, *turned))
    other = swap(own[:, :, 4 * head :], 1)
    parity = core.reshape(1)
    columns = turned[:1] + [swap(turned[d], (d & 1) * 2 + (d >> 1) * 8) for d in range(1, 4)]

    scores, dk, dv_mine, dv_theirs = value_gradients(parity, own, other)
    values = pack_values(dv_mine, swap(dv_theirs, 1))
    values, own, *columns = lax.optimization_barrier((values, own, *columns))
    values_back = across(values)

    scores, dk_mine, dk_theirs = score_gradients(parity, own, other, scores, dk)
    scores = pack_scores(scores, dk_mine, swap(dk_theirs, 1))
    values_back, scores = lax.optimization_barrier((values_back, scores))
    scores_back = across(scores)
    give, keep, value_gradient = input_product(place, columns, values_back)
    got = swap(give, 1)

    keep = keep.reshape(2, 2, -1, width)
    got = got.reshape(keep.shape)
    sections = lax.axis_size("section")
    cross_other, cross_own, stay_other, second_own, first_own = cut_pieces(place, keep, got)

    def routed(block, route, group):
        axes = ("section", "ctx", "mirror")
        pairs = [
            ((s * 2 * chips + i) * 2 + m, (t * 2 * chips + (i ^ group)) * 2 + n)
            for (s, m), (t, n) in route
            for i in range(2 * chips)
        ]
        return lax.ppermute(block, axes, pairs)

    far = [((s, 1), (sections - 1 - s, 1)) for s in range(sections)]
    cross = [((s, 1), (sections - 1 - s, 0)) for s in range(sections)]
    cross += [((s, 0), (s, 1)) for s in range(sections)]
    near_other = routed(cross_other, cross, 4)
    other = routed(stay_other, far + [((s, 0), (s, 0)) for s in range(sections)], 4)
    cross_own, second_own, scores_back = lax.optimization_barrier((cross_own, second_own, scores_back))
    near_own = routed(cross_own, cross, 0)
    far_own = routed(second_own, far, 0)
    rotated = finish(
        place,
        hadamard_signs,
        jnp.asarray(hadamard(width), jnp.bfloat16),
        (first_own, near_other, near_own, far_own, other),
    )
    query_gradient, key_gradient = unpack_scores(scores_back)
    return (
        query_gradient[None, None],
        key_gradient[None, None],
        value_gradient[None, None],
        rotated[None],
    )


def solution(mesh):
    split = P("section", "mirror", "ctx", None)
    return jax.shard_map(
        body,
        mesh=mesh,
        in_specs=(split, split, split, split, split, P()),
        out_specs=(split, split, split, P("section", ("ctx", "mirror"), None)),
        check_vma=False,
    )
```

```python
import math

import jax
import jax.numpy as jnp
import numpy as np
from jax import lax
from jax.experimental import pallas as pl
from jax.experimental.pallas import tpu as pltpu
from jax.sharding import PartitionSpec as P

KEY_VALUE_HEADS = 8
HEAD_SIZE = 128
WINDOW = 2048
SCORE_SCALE = 144.0 ** (-0.5)
SOFTCAP = 50.0
LOG2E = math.log2(math.e)
WHOLE = pl.BlockSpec(memory_space=pltpu.VMEM)
SCALAR = pl.BlockSpec(memory_space=pltpu.SMEM)


def dot(a, b, contract):
    return lax.dot_general(
        a, b, ((contract[:1], contract[1:]), ((), ())), preferred_element_type=jnp.float32
    )


def pair(ref, first):
    at = first * HEAD_SIZE
    return jnp.concatenate(
        [ref[0, :, at : at + HEAD_SIZE], ref[0, :, at + HEAD_SIZE : at + 2 * HEAD_SIZE]],
        axis=0,
    )


def full_window(span):
    return ["far"] + ["middle"] * (span - 1) + ["near"]


def early_windows(step, parity, span, one):
    block = 2 * step + parity
    for early in range(span // 2):

        @pl.when(step == early)
        def _():
            distance = 2 * early
            one(
                [
                    (jnp.maximum(block - distance - 1, 0), 0, ["maybe"]),
                    (block - distance, 1, ["middle"] * distance + ["near"]),
                ]
            )


def weights(s, kind, parity):
    rows = s.shape[0]
    capped = jnp.tanh(s * (SCORE_SCALE / SOFTCAP))
    e = jnp.exp2(capped * (SOFTCAP * LOG2E))
    if kind == "maybe":
        e = jnp.where(parity == 1, e, 0.0)
    elif kind != "middle":
        key_place = lax.broadcasted_iota(jnp.int32, s.shape, 0)
        query_place = lax.broadcasted_iota(jnp.int32, s.shape, 1) % rows
        allowed = key_place <= query_place if kind == "near" else key_place > query_place
        e = jnp.where(allowed, e, 0.0)
    return capped, e


def blocks_at(ref, place, kinds):
    block = ref[pl.ds(place, len(kinds))]
    return block.reshape(len(kinds) * block.shape[1], block.shape[2])


def column_sums(x):
    return jnp.sum(x.reshape(x.shape[0] // 8, 8, x.shape[1]), axis=0)


def turned_rows(x, scale):
    scale = jnp.transpose(jnp.broadcast_to(scale, (x.shape[1], x.shape[0])))
    return (x.astype(jnp.float32) * scale).astype(jnp.bfloat16)


def store_query_gradient(ref, turned):
    rows = turned.shape[1] // 2
    dq = jnp.transpose(turned).astype(jnp.bfloat16)
    ref[0, :, : turned.shape[0]] = dq[:rows]
    ref[0, :, turned.shape[0] :] = dq[rows:]


def value_kernel(
    parity_ref,
    own_ref,
    own_kv_ref,
    other_ref,
    dq_ref,
    dk_ref,
    mine_ref,
    theirs_ref,
    k_s,
    v_s,
    kt_s,
    dv_s,
    e_s,
    u_s,
    dp_s,
):
    chips, rows, _ = own_kv_ref.shape
    span = WINDOW // rows
    head = HEAD_SIZE
    parity = parity_ref[0]
    step = pl.program_id(0)
    block = 2 * step + parity

    @pl.when(step == 0)
    def _():
        @pl.loop(0, chips)
        def _(j):
            k_s[2 * j + parity] = own_kv_ref[j, :, :head]
            k_s[2 * j + 1 - parity] = other_ref[j, :, :head]

        @pl.loop(0, span // 2)
        def _(j):
            v_s[2 * j + parity] = own_kv_ref[j, :, head:]
            v_s[2 * j + 1 - parity] = other_ref[j, :, head:]

        @pl.loop(0, span)
        def _(j):
            kt_s[j] = jnp.transpose(k_s[j])

        dv_s[...] = jnp.zeros_like(dv_s)
        dk_ref[...] = jnp.zeros_like(dk_ref)

    q2 = pair(own_ref, 0)
    g2 = pair(own_ref, 2)

    def early(runs):
        sums = jnp.zeros((8, 2 * rows), jnp.float32)
        products = jnp.zeros((8, 2 * rows), jnp.float32)
        for place, slot, kinds in runs:
            s = dot(blocks_at(k_s, place, kinds), q2, (1, 1))
            dps = dot(blocks_at(v_s, place, kinds), g2, (1, 1))
            for i, kind in enumerate(kinds):
                capped, e = weights(s[i * rows : (i + 1) * rows], kind, parity)
                dp = dps[i * rows : (i + 1) * rows]
                sums = sums + column_sums(e)
                products = products + column_sums(e * dp)
                e_s[slot + i] = e.astype(jnp.bfloat16)
                u_s[slot + i] = (e - e * (capped * capped)).astype(jnp.bfloat16)
                dp_s[slot + i] = dp
        inverse = 1.0 / jnp.sum(sums, axis=0, keepdims=True)
        delta = jnp.sum(products, axis=0, keepdims=True) * inverse
        g2_scaled = turned_rows(g2, inverse)
        q2_scaled = turned_rows(q2, inverse * SCORE_SCALE)
        turned = jnp.zeros((head, 2 * rows), jnp.float32)
        for place, slot, kinds in runs:
            n = len(kinds)
            grad = [
                u_s[slot + i] * (dp_s[slot + i] - delta).astype(jnp.bfloat16) for i in range(n)
            ]
            grad = jnp.concatenate(grad, axis=0)
            term = dot(blocks_at(e_s, slot, kinds), g2_scaled, (1, 0))
            dv_s[pl.ds(place, n)] += term.reshape(n, rows, head)
            dk_ref[pl.ds(place, n)] += dot(grad, q2_scaled, (1, 0)).reshape(n, rows, head)
            keys = jnp.concatenate([kt_s[place + i] for i in range(n)], axis=1)
            turned = turned + dot(keys, grad, (1, 0))
        store_query_gradient(dq_ref, turned * (inverse * SCORE_SCALE))

    early_windows(step, parity, span, early)

    @pl.when(step >= span // 2)
    def _():
        kinds = full_window(span)
        place = block - span
        s = dot(blocks_at(k_s, place, kinds), q2, (1, 1))
        sums = jnp.zeros((8, 2 * rows), jnp.float32)
        for i, kind in enumerate(kinds):
            _, e = weights(s[i * rows : (i + 1) * rows], kind, parity)
            sums = sums + column_sums(e)
            e_s[i] = e.astype(jnp.bfloat16)
        g2_scaled = turned_rows(g2, 1.0 / jnp.sum(sums, axis=0, keepdims=True))
        term = dot(blocks_at(e_s, 0, kinds), g2_scaled, (1, 0))
        dv_s[pl.ds(place, span + 1)] += term.reshape(span + 1, rows, head)

    @pl.when(step == chips - 1)
    def _():
        @pl.loop(0, chips)
        def _(j):
            mine_ref[j] = dv_s[2 * j + parity].astype(jnp.bfloat16)
            theirs_ref[j] = dv_s[2 * j + 1 - parity].astype(jnp.bfloat16)


def score_kernel(
    parity_ref,
    own_ref,
    own_kv_ref,
    other_ref,
    _,
    dk_ref,
    dq_ref,
    mine_ref,
    theirs_ref,
    k_s,
    v_s,
    kt_s,
    dk_s,
    u_s,
    dp_s,
):
    chips, rows, _ = own_kv_ref.shape
    span = WINDOW // rows
    head = HEAD_SIZE
    parity = parity_ref[0]
    step = pl.program_id(0)
    place = 2 * (step + span // 2) + parity - span

    @pl.when(step == 0)
    def _():
        @pl.loop(0, chips)
        def _(j):
            mine, theirs = 2 * j + parity, 2 * j + 1 - parity
            for to, k, v in (
                (mine, own_kv_ref[j, :, :head], own_kv_ref[j, :, head:]),
                (theirs, other_ref[j, :, :head], other_ref[j, :, head:]),
            ):
                k_s[to] = k
                v_s[to] = v
                kt_s[to] = jnp.transpose(k)

        dk_s[:span] = dk_ref[...]
        dk_s[span:] = jnp.zeros((2 * chips - span, rows, head), jnp.float32)

    q2 = pair(own_ref, 0)
    g2 = pair(own_ref, 2)
    kinds = full_window(span)
    s = dot(blocks_at(k_s, place, kinds), q2, (1, 1))
    dps = dot(blocks_at(v_s, place, kinds), g2, (1, 1))
    sums = jnp.zeros((8, 2 * rows), jnp.float32)
    products = jnp.zeros((8, 2 * rows), jnp.float32)
    for i, kind in enumerate(kinds):
        capped, e = weights(s[i * rows : (i + 1) * rows], kind, parity)
        dp = dps[i * rows : (i + 1) * rows]
        sums = sums + column_sums(e)
        products = products + column_sums(e * dp)
        u_s[i] = (e - e * (capped * capped)).astype(jnp.bfloat16)
        dp_s[i] = dp
    inverse = 1.0 / jnp.sum(sums, axis=0, keepdims=True)
    delta = jnp.sum(products, axis=0, keepdims=True) * inverse
    q2_scaled = turned_rows(q2, inverse * SCORE_SCALE)
    grad = [u_s[i] * (dp_s[i] - delta).astype(jnp.bfloat16) for i in range(span + 1)]
    grad = jnp.concatenate(grad, axis=0)
    dk_s[pl.ds(place, span + 1)] += dot(grad, q2_scaled, (1, 0)).reshape(span + 1, rows, head)
    keys = jnp.concatenate([kt_s[place + i] for i in range(span + 1)], axis=1)
    store_query_gradient(dq_ref, dot(keys, grad, (1, 0)) * (inverse * SCORE_SCALE))

    @pl.when(step == chips - span // 2 - 1)
    def _():
        @pl.loop(0, chips)
        def _(j):
            mine_ref[j] = dk_s[2 * j + parity].astype(jnp.bfloat16)
            theirs_ref[j] = dk_s[2 * j + 1 - parity].astype(jnp.bfloat16)


def attention_call(kernel, name, operands, first, more_in, more_out, scratch, products, vmem):
    chips, rows, _ = operands[1].shape
    head = HEAD_SIZE
    early = WINDOW // rows // 2
    grads = jax.ShapeDtypeStruct((chips, rows, head), jnp.bfloat16)
    payload = jax.ShapeDtypeStruct((chips, rows, 3 * head), jnp.bfloat16)

    def query_block(t):
        return (t + first if first else jnp.minimum(t, early - 1), 0, 0)

    return pl.pallas_call(
        kernel,
        grid=(chips - first,),
        out_shape=[payload] + [shape for shape, _ in more_out] + [grads, grads],
        in_specs=[
            SCALAR,
            pl.BlockSpec((1, rows, 4 * head), lambda t: (t + first, 0, 0)),
            pl.BlockSpec((chips, rows, 2 * head), lambda t: (0, 0, 2), pipeline_mode=pl.Buffered(1)),
            WHOLE,
        ]
        + more_in,
        out_specs=[pl.BlockSpec((1, rows, 2 * head), query_block)]
        + [spec for _, spec in more_out]
        + [WHOLE, WHOLE],
        scratch_shapes=[pltpu.VMEM(shape, kind) for shape, kind in scratch],
        input_output_aliases={4: 0} if first else {},
        compiler_params=pltpu.CompilerParams(
            dimension_semantics=("arbitrary",), vmem_limit_bytes=vmem * 2**20
        ),
        cost_estimate=pl.CostEstimate(
            flops=2 * products * 112 * rows * rows * head,
            bytes_accessed=8 * 2**20,
            transcendentals=2 * 112 * rows * rows,
        ),
        name=name,
    )(*operands)


def value_gradients(parity, own, other):
    chips, rows, _ = own.shape
    span = WINDOW // rows
    head = HEAD_SIZE
    dk = jax.ShapeDtypeStruct((span, rows, head), jnp.float32)
    return attention_call(
        value_kernel,
        "value_gradients",
        (parity, own, own, other),
        0,
        [],
        [(dk, WHOLE)],
        [
            ((2 * chips, rows, head), jnp.bfloat16),
            ((span, rows, head), jnp.bfloat16),
            ((span, head, rows), jnp.bfloat16),
            ((2 * chips, rows, head), jnp.float32),
            ((span + 1, rows, 2 * rows), jnp.bfloat16),
            ((span, rows, 2 * rows), jnp.bfloat16),
            ((span, rows, 2 * rows), jnp.float32),
        ],
        4,
        28,
    )


def score_gradients(parity, own, other, payload, dk):
    chips, rows, _ = own.shape
    span = WINDOW // rows
    head = HEAD_SIZE
    return attention_call(
        score_kernel,
        "score_gradients",
        (parity, own, own, other, payload, dk),
        span // 2,
        [pl.BlockSpec(memory_space=pl.ANY), WHOLE],
        [],
        [
            ((2 * chips, rows, head), jnp.bfloat16),
            ((2 * chips, rows, head), jnp.bfloat16),
            ((2 * chips, head, rows), jnp.bfloat16),
            ((2 * chips, rows, head), jnp.float32),
            ((span + 1, rows, 2 * rows), jnp.bfloat16),
            ((span + 1, rows, 2 * rows), jnp.float32),
        ],
        8,
        60,
    )


def small_call(
    kernel,
    name,
    out_shape,
    scratch,
    flops,
    *operands,
    grid=None,
    in_specs=None,
    out_specs=None,
    kind=jnp.bfloat16,
    vmem=16,
    aliases=None,
    moved=None,
):
    kinds = [jax.ShapeDtypeStruct(shape, kind) for shape in out_shape]
    specs = {}
    if grid is not None:
        specs = {"grid": grid}
    if moved is None:
        moved = sum(2 * x.size for x in operands) + sum(2 * math.prod(s) for s in out_shape)
    return pl.pallas_call(
        kernel,
        out_shape=kinds,
        in_specs=in_specs if in_specs is not None else [WHOLE] * len(operands),
        out_specs=out_specs if out_specs is not None else [WHOLE] * len(kinds),
        scratch_shapes=scratch,
        compiler_params=pltpu.CompilerParams(vmem_limit_bytes=vmem * 2**20),
        cost_estimate=pl.CostEstimate(flops=flops, bytes_accessed=moved, transcendentals=0),
        name=name,
        input_output_aliases=aliases or {},
        **specs,
    )(*operands)


def pack_heads(queries, output_gradient, saved_keys, saved_values):
    heads = KEY_VALUE_HEADS

    def kernel(*refs):
        out_ref, at = refs[-1], 0
        for ref in refs[:-1]:
            wide = ref.shape[1] // heads
            for g in range(heads):
                out_ref[g, :, at : at + wide] = ref[:, g * wide : (g + 1) * wide]
            at += wide

    rows = queries.shape[0]
    arrays = (queries, output_gradient, saved_keys, saved_values)
    part = rows // 2
    total = sum(x.shape[1] for x in arrays) // heads
    (packed,) = small_call(
        kernel,
        "pack_heads",
        [(heads, rows, total)],
        [],
        0,
        *arrays,
        grid=(rows // part,),
        in_specs=[pl.BlockSpec((part, x.shape[1]), lambda r: (r, 0)) for x in arrays],
        out_specs=[pl.BlockSpec((heads, part, total), lambda r: (0, r, 0))],
        vmem=60,
    )
    return packed


def pack_scores(payload, mine, theirs):
    def kernel(_, mine_ref, theirs_ref, out_ref):
        out_ref[...] = add(mine_ref[...], theirs_ref[...])

    chips, rows, head = mine.shape
    part = chips // 2
    block = pl.BlockSpec((part, rows, head), lambda t: (t, 0, 0))
    (packed,) = small_call(
        kernel,
        "pack_scores",
        [payload.shape],
        [],
        0,
        payload,
        mine,
        theirs,
        grid=(chips // part,),
        in_specs=[pl.BlockSpec(memory_space=pl.ANY), block, block],
        out_specs=[pl.BlockSpec((part, rows, head), lambda t: (t, 0, 2))],
        vmem=60,
        aliases={0: 0},
    )
    return packed


def unpack_scores(back):
    def kernel(in_ref, dq_ref, dk_ref):
        for g in range(heads):
            dq_ref[:, g * 2 * head : (g + 1) * 2 * head] = in_ref[g, :, : 2 * head]
            dk_ref[:, g * head : (g + 1) * head] = in_ref[g, :, 2 * head :]

    heads, rows, width = back.shape
    head = HEAD_SIZE
    part = rows // 4
    widths = (2 * head * heads, head * heads)
    return small_call(
        kernel,
        "unpack_scores",
        [(rows, w) for w in widths],
        [],
        0,
        back,
        grid=(rows // part,),
        in_specs=[pl.BlockSpec((heads, part, width), lambda r: (0, r, 0))],
        out_specs=[pl.BlockSpec((part, w), lambda r: (r, 0)) for w in widths],
    )


def pack_values(mine, theirs):
    def kernel(mine_ref, theirs_ref, out_ref):
        for x in range(2):
            for y in range(2):
                total = add(mine_ref[x, y, 0], theirs_ref[x, y, 0])
                for to in range(4):
                    out_ref[to // 2, to % 2, 0, 2 * x + y] = total

    chips, rows, head = mine.shape
    split = (2, 2, 2, rows, head)
    (packed,) = small_call(
        kernel,
        "pack_values",
        [split[:3] + (4, rows, head)],
        [],
        0,
        mine.reshape(split),
        theirs.reshape(split),
        grid=(2,),
        in_specs=[pl.BlockSpec((2, 2, 1, rows, head), lambda p: (0, 0, p, 0, 0))] * 2,
        out_specs=[pl.BlockSpec((2, 2, 1, 4, rows, head), lambda p: (0, 0, p, 0, 0, 0))],
        vmem=16,
    )
    return packed.reshape(chips, 4, rows, head)


def turn_input(place, input_rows):
    rows, depth = input_rows.shape
    share = depth // 16
    wide = 2 * HEAD_SIZE

    def kernel(place_ref, in_ref, *refs):
        out_refs, turned_s = refs[:-1], refs[-1]
        for at in range(0, depth, wide):
            turned_s[at : at + wide] = jnp.transpose(in_ref[:, at : at + wide])
        for distance, out_ref in enumerate(out_refs):
            to = place_ref[0] ^ distance
            for core in range(2):
                for group in range(2):
                    high = to % 2 if group else to % 2 ^ core
                    low = place_ref[2] if group else 1 - place_ref[2]
                    index = ((to // 2 * 2 + high) * 2 + low) * 2 + core
                    piece = turned_s[pl.ds(pl.multiple_of(index * share, 16), share)]
                    out_ref[group, core * share : (core + 1) * share] = piece

    return small_call(
        kernel,
        "turn_input",
        [(2, 2 * share, rows)] * 4,
        [pltpu.VMEM((depth, rows), jnp.bfloat16)],
        0,
        place,
        input_rows,
        in_specs=[SCALAR, WHOLE],
    )


def input_product(place, columns, back):
    members = len(columns)
    heads, _, rows, head = back.shape
    share = columns[0].shape[1] // 2

    def kernel(place_ref, *refs):
        column_refs, back_ref = refs[:members], refs[members]
        give_ref, keep_ref, value_ref = refs[members + 1 :]
        member, core = place_ref[0], place_ref[1]
        v = [
            jnp.concatenate([back_ref[0, member ^ d], back_ref[1, member ^ d]], axis=1)
            for d in range(members)
        ]
        value_ref[...] = v[0]
        v = jnp.concatenate(v, axis=0)
        for at in range(2):
            for out_ref, which_core in ((give_ref, 1 - core), (keep_ref, core)):
                part = pl.ds(pl.multiple_of(which_core * share, 16), share)
                x = jnp.concatenate([ref[at, part] for ref in column_refs], axis=1)
                out_ref[at] = dot(x, v, (1, 0)).astype(jnp.bfloat16)

    once = pl.Buffered(1)
    halves = pl.BlockSpec((2, share, 2 * head), lambda g: (0, 0, g))
    return small_call(
        kernel,
        "input_product",
        [(2, share, heads * head)] * 2 + [(rows, heads * head)],
        [],
        0,
        place,
        *columns,
        back,
        grid=(heads // 2,),
        in_specs=[SCALAR]
        + [pl.BlockSpec((2, 2 * share, rows), lambda g: (0, 0, 0), pipeline_mode=once)] * members
        + [pl.BlockSpec((2, members, rows, head), lambda g: (g, 0, 0, 0))],
        out_specs=[halves, halves, pl.BlockSpec((rows, 2 * head), lambda g: (0, g))],
        vmem=60,
        moved=0,
    )


def add32(a, b):
    return a.astype(jnp.float32) + b.astype(jnp.float32)


def add(a, b):
    return add32(a, b).astype(jnp.bfloat16)


def cut_pieces(place, keep, got):
    def kernel(place_ref, keep_ref, got_ref, cross_other_ref, cross_own_ref, stay_ref, second_ref, own_ref):
        mirror = place_ref[3]
        cross_other_ref[...] = add(keep_ref[0, 1 - mirror], got_ref[0, 1 - mirror])
        cross_own_ref[...] = add(keep_ref[1, 1 - mirror], got_ref[1, 1 - mirror])
        stay_ref[...] = add(keep_ref[0, mirror], got_ref[0, mirror])
        second_ref[...] = add(keep_ref[1, 1], got_ref[1, 1])
        own_ref[...] = add(keep_ref[1, 0], got_ref[1, 0])

    return small_call(
        kernel,
        "cut_pieces",
        [keep.shape[2:]] * 5,
        [],
        0,
        place,
        keep,
        got,
        in_specs=[SCALAR, WHOLE, WHOLE],
    )


def finish(place, turn, pieces):
    def kernel(place_ref, turn_ref, own_ref, near_ref, near2_ref, far_ref, other_ref, out_ref):
        total = jnp.where(place_ref[3] == 0, own_ref[...], far_ref[...]).astype(jnp.float32)
        total = total + add32(near_ref[...], near2_ref[...]) + other_ref[...].astype(jnp.float32)
        out_ref[...] = dot(total.astype(jnp.bfloat16), turn_ref[...], (1, 0))

    own = pieces[0]
    (out,) = small_call(
        kernel,
        "finish",
        [own.shape],
        [],
        2 * own.size * own.shape[1],
        place,
        turn,
        *pieces,
        in_specs=[SCALAR] + [WHOLE] * 6,
        kind=jnp.float32,
    )
    return out


def hadamard(order_size):
    place = np.arange(order_size)
    both = place[:, None] & place[None, :]
    parity = np.zeros_like(both)
    for bit in range(order_size.bit_length() - 1):
        parity ^= both >> bit & 1
    return (1 - 2 * parity) / math.sqrt(order_size)


def body(queries, saved_keys, saved_values, output_gradient, layer_input, hadamard_signs):
    width = saved_keys.shape[3]
    head = HEAD_SIZE
    chips = lax.axis_size("ctx") // 2
    sections = lax.axis_size("section")
    ctx = lax.axis_index("ctx").astype(jnp.int32)
    section = lax.axis_index("section").astype(jnp.int32)
    mirror = lax.axis_index("mirror").astype(jnp.int32)
    core = ctx & 1
    same_core = [[2 * chip + c for chip in range(chips)] for c in range(2)]
    member = (ctx >> 3) * 2 + (ctx >> 2 & 1)
    place = jnp.stack([member, core, ctx >> 1 & 1, mirror])

    def across(block):
        return lax.all_to_all(block, "ctx", 0, 0, tiled=True, axis_index_groups=same_core)

    def swap(block, bits):
        return lax.ppermute(block, "ctx", [(i, i ^ bits) for i in range(2 * chips)])

    turned = turn_input(place, layer_input[0, 0])
    own = across(
        pack_heads(queries[0, 0], output_gradient[0, 0], saved_keys[0, 0], saved_values[0, 0])
    )
    own, *turned = lax.optimization_barrier((own, *turned))
    other = swap(own[:, :, 4 * head :], 1)
    parity = core.reshape(1)
    columns = turned[:1] + [swap(turned[d], (d & 1) * 4 + (d >> 1) * 8) for d in range(1, 4)]

    scores, dk, dv_mine, dv_theirs = value_gradients(parity, own, other)
    values = pack_values(dv_mine, swap(dv_theirs, 1))
    values, own, *columns = lax.optimization_barrier((values, own, *columns))
    values_back = across(values)

    scores, dk_mine, dk_theirs = score_gradients(parity, own, other, scores, dk)
    scores = pack_scores(scores, dk_mine, swap(dk_theirs, 1))
    values_back, scores = lax.optimization_barrier((values_back, scores))
    scores_back = across(scores)
    give, keep, value_gradient = input_product(place, columns, values_back)
    got = swap(give, 1)

    keep = keep.reshape(2, 2, -1, width)
    got = got.reshape(keep.shape)
    sections = lax.axis_size("section")
    cross_other, cross_own, stay_other, second_own, first_own = cut_pieces(place, keep, got)

    def routed(block, route, groups):
        axes = ("section", "ctx", "mirror")
        pairs = [
            ((s * 2 * chips + i) * 2 + m, (t * 2 * chips + (i ^ groups[i % 2])) * 2 + n)
            for (s, m), (t, n) in route
            for i in range(2 * chips)
        ]
        return lax.ppermute(block, axes, pairs)

    far = [((s, 1), (sections - 1 - s, 1)) for s in range(sections)]
    cross = [((s, 1), (sections - 1 - s, 0)) for s in range(sections)]
    cross += [((s, 0), (s, 1)) for s in range(sections)]
    near_other = routed(cross_other, cross, (2, 6))
    other = routed(stay_other, far + [((s, 0), (s, 0)) for s in range(sections)], (2, 6))
    cross_own, second_own, scores_back = lax.optimization_barrier((cross_own, second_own, scores_back))
    near_own = routed(cross_own, cross, (0, 0))
    far_own = routed(second_own, far, (0, 0))
    signs = lax.dynamic_index_in_dim(hadamard_signs, section, 0, keepdims=False)
    turn = jnp.asarray(hadamard(width), jnp.bfloat16) * signs.astype(jnp.bfloat16)[:, None]
    rotated = finish(
        place,
        turn,
        (first_own, near_other, near_own, far_own, other),
    )
    query_gradient, key_gradient = unpack_scores(scores_back)
    return (
        query_gradient[None, None],
        key_gradient[None, None],
        value_gradient[None, None],
        rotated[None],
    )


def solution(mesh):
    split = P("section", "mirror", "ctx", None)
    return jax.shard_map(
        body,
        mesh=mesh,
        in_specs=(split, split, split, split, split, P()),
        out_specs=(split, split, split, P("section", ("ctx", "mirror"), None)),
        check_vma=False,
    )
```

```python
import math

import jax
import jax.numpy as jnp
import numpy as np
from jax import lax
from jax.experimental import pallas as pl
from jax.experimental.pallas import tpu as pltpu
from jax.sharding import PartitionSpec as P

KEY_VALUE_HEADS = 8
HEAD_SIZE = 128
WINDOW = 2048
SCORE_SCALE = 144.0 ** (-0.5)
SOFTCAP = 50.0
LOG2E = math.log2(math.e)
WHOLE = pl.BlockSpec(memory_space=pltpu.VMEM)
SCALAR = pl.BlockSpec(memory_space=pltpu.SMEM)


def dot(a, b, contract):
    return lax.dot_general(
        a, b, ((contract[:1], contract[1:]), ((), ())), preferred_element_type=jnp.float32
    )


def pair(ref, first):
    at = first * HEAD_SIZE
    return jnp.concatenate(
        [ref[0, :, at : at + HEAD_SIZE], ref[0, :, at + HEAD_SIZE : at + 2 * HEAD_SIZE]],
        axis=0,
    )


def full_window(span):
    return ["far"] + ["middle"] * (span - 1) + ["near"]


def early_windows(step, parity, span, one):
    block = 2 * step + parity
    for early in range(span // 2):

        @pl.when(step == early)
        def _():
            distance = 2 * early
            one(
                [
                    (jnp.maximum(block - distance - 1, 0), 0, ["maybe"]),
                    (block - distance, 1, ["middle"] * distance + ["near"]),
                ]
            )


def weights(s, kind, parity):
    rows = s.shape[0]
    capped = jnp.tanh(s * (SCORE_SCALE / SOFTCAP))
    e = jnp.exp2(capped * (SOFTCAP * LOG2E))
    if kind == "maybe":
        e = jnp.where(parity == 1, e, 0.0)
    elif kind != "middle":
        key_place = lax.broadcasted_iota(jnp.int32, s.shape, 0)
        query_place = lax.broadcasted_iota(jnp.int32, s.shape, 1) % rows
        allowed = key_place <= query_place if kind == "near" else key_place > query_place
        e = jnp.where(allowed, e, 0.0)
    return capped, e


def blocks_at(ref, place, kinds):
    block = ref[pl.ds(place, len(kinds))]
    return block.reshape(len(kinds) * block.shape[1], block.shape[2])


def column_sums(x):
    return jnp.sum(x.reshape(x.shape[0] // 8, 8, x.shape[1]), axis=0)


def turned_rows(x, scale):
    scale = jnp.transpose(jnp.broadcast_to(scale, (x.shape[1], x.shape[0])))
    return (x.astype(jnp.float32) * scale).astype(jnp.bfloat16)


def store_query_gradient(ref, turned):
    rows = turned.shape[1] // 2
    dq = jnp.transpose(turned).astype(jnp.bfloat16)
    ref[0, :, : turned.shape[0]] = dq[:rows]
    ref[0, :, turned.shape[0] :] = dq[rows:]


def value_kernel(
    parity_ref,
    own_ref,
    own_kv_ref,
    other_ref,
    dq_ref,
    dk_ref,
    mine_ref,
    theirs_ref,
    k_s,
    v_s,
    kt_s,
    dv_s,
    e_s,
    u_s,
    dp_s,
):
    chips, rows, _ = own_kv_ref.shape
    span = WINDOW // rows
    head = HEAD_SIZE
    parity = parity_ref[0]
    step = pl.program_id(0)
    block = 2 * step + parity

    @pl.when(step == 0)
    def _():
        @pl.loop(0, chips)
        def _(j):
            k_s[2 * j + parity] = own_kv_ref[j, :, :head]
            k_s[2 * j + 1 - parity] = other_ref[j, :, :head]

        @pl.loop(0, span // 2)
        def _(j):
            v_s[2 * j + parity] = own_kv_ref[j, :, head:]
            v_s[2 * j + 1 - parity] = other_ref[j, :, head:]

        @pl.loop(0, span)
        def _(j):
            kt_s[j] = jnp.transpose(k_s[j])

        dv_s[...] = jnp.zeros_like(dv_s)
        dk_ref[...] = jnp.zeros_like(dk_ref)

    q2 = pair(own_ref, 0)
    g2 = pair(own_ref, 2)

    def early(runs):
        sums = jnp.zeros((8, 2 * rows), jnp.float32)
        products = jnp.zeros((8, 2 * rows), jnp.float32)
        for place, slot, kinds in runs:
            s = dot(blocks_at(k_s, place, kinds), q2, (1, 1))
            dps = dot(blocks_at(v_s, place, kinds), g2, (1, 1))
            for i, kind in enumerate(kinds):
                capped, e = weights(s[i * rows : (i + 1) * rows], kind, parity)
                dp = dps[i * rows : (i + 1) * rows]
                sums = sums + column_sums(e)
                products = products + column_sums(e * dp)
                e_s[slot + i] = e.astype(jnp.bfloat16)
                u_s[slot + i] = (e - e * (capped * capped)).astype(jnp.bfloat16)
                dp_s[slot + i] = dp
        inverse = 1.0 / jnp.sum(sums, axis=0, keepdims=True)
        delta = jnp.sum(products, axis=0, keepdims=True) * inverse
        g2_scaled = turned_rows(g2, inverse)
        q2_scaled = turned_rows(q2, inverse * SCORE_SCALE)
        turned = jnp.zeros((head, 2 * rows), jnp.float32)
        for place, slot, kinds in runs:
            n = len(kinds)
            grad = [
                u_s[slot + i] * (dp_s[slot + i] - delta).astype(jnp.bfloat16) for i in range(n)
            ]
            grad = jnp.concatenate(grad, axis=0)
            term = dot(blocks_at(e_s, slot, kinds), g2_scaled, (1, 0))
            dv_s[pl.ds(place, n)] += term.reshape(n, rows, head)
            dk_ref[pl.ds(place, n)] += dot(grad, q2_scaled, (1, 0)).reshape(n, rows, head)
            keys = jnp.concatenate([kt_s[place + i] for i in range(n)], axis=1)
            turned = turned + dot(keys, grad, (1, 0))
        store_query_gradient(dq_ref, turned * (inverse * SCORE_SCALE))

    early_windows(step, parity, span, early)

    @pl.when(step >= span // 2)
    def _():
        kinds = full_window(span)
        place = block - span
        s = dot(blocks_at(k_s, place, kinds), q2, (1, 1))
        sums = jnp.zeros((8, 2 * rows), jnp.float32)
        for i, kind in enumerate(kinds):
            _, e = weights(s[i * rows : (i + 1) * rows], kind, parity)
            sums = sums + column_sums(e)
            e_s[i] = e.astype(jnp.bfloat16)
        g2_scaled = turned_rows(g2, 1.0 / jnp.sum(sums, axis=0, keepdims=True))
        term = dot(blocks_at(e_s, 0, kinds), g2_scaled, (1, 0))
        dv_s[pl.ds(place, span + 1)] += term.reshape(span + 1, rows, head)

    @pl.when(step == chips - 1)
    def _():
        @pl.loop(0, chips)
        def _(j):
            mine_ref[j] = dv_s[2 * j + parity].astype(jnp.bfloat16)
            theirs_ref[j] = dv_s[2 * j + 1 - parity].astype(jnp.bfloat16)


def score_kernel(
    parity_ref,
    own_ref,
    own_kv_ref,
    other_ref,
    _,
    dk_ref,
    dq_ref,
    mine_ref,
    theirs_ref,
    k_s,
    v_s,
    kt_s,
    dk_s,
    u_s,
    dp_s,
):
    chips, rows, _ = own_kv_ref.shape
    span = WINDOW // rows
    head = HEAD_SIZE
    parity = parity_ref[0]
    step = pl.program_id(0)
    place = 2 * (step + span // 2) + parity - span

    @pl.when(step == 0)
    def _():
        @pl.loop(0, chips)
        def _(j):
            mine, theirs = 2 * j + parity, 2 * j + 1 - parity
            for to, k, v in (
                (mine, own_kv_ref[j, :, :head], own_kv_ref[j, :, head:]),
                (theirs, other_ref[j, :, :head], other_ref[j, :, head:]),
            ):
                k_s[to] = k
                v_s[to] = v
                kt_s[to] = jnp.transpose(k)

        dk_s[:span] = dk_ref[...]
        dk_s[span:] = jnp.zeros((2 * chips - span, rows, head), jnp.float32)

    q2 = pair(own_ref, 0)
    g2 = pair(own_ref, 2)
    kinds = full_window(span)
    s = dot(blocks_at(k_s, place, kinds), q2, (1, 1))
    dps = dot(blocks_at(v_s, place, kinds), g2, (1, 1))
    sums = jnp.zeros((8, 2 * rows), jnp.float32)
    products = jnp.zeros((8, 2 * rows), jnp.float32)
    for i, kind in enumerate(kinds):
        capped, e = weights(s[i * rows : (i + 1) * rows], kind, parity)
        dp = dps[i * rows : (i + 1) * rows]
        sums = sums + column_sums(e)
        products = products + column_sums(e * dp)
        u_s[i] = (e - e * (capped * capped)).astype(jnp.bfloat16)
        dp_s[i] = dp
    inverse = 1.0 / jnp.sum(sums, axis=0, keepdims=True)
    delta = jnp.sum(products, axis=0, keepdims=True) * inverse
    q2_scaled = turned_rows(q2, inverse * SCORE_SCALE)
    grad = [u_s[i] * (dp_s[i] - delta).astype(jnp.bfloat16) for i in range(span + 1)]
    grad = jnp.concatenate(grad, axis=0)
    dk_s[pl.ds(place, span + 1)] += dot(grad, q2_scaled, (1, 0)).reshape(span + 1, rows, head)
    keys = jnp.concatenate([kt_s[place + i] for i in range(span + 1)], axis=1)
    store_query_gradient(dq_ref, dot(keys, grad, (1, 0)) * (inverse * SCORE_SCALE))

    @pl.when(step == chips - span // 2 - 1)
    def _():
        @pl.loop(0, chips)
        def _(j):
            mine_ref[j] = dk_s[2 * j + parity].astype(jnp.bfloat16)
            theirs_ref[j] = dk_s[2 * j + 1 - parity].astype(jnp.bfloat16)


def attention_call(kernel, name, operands, first, more_in, more_out, scratch, products, vmem):
    chips, rows, _ = operands[1].shape
    head = HEAD_SIZE
    early = WINDOW // rows // 2
    grads = jax.ShapeDtypeStruct((chips, rows, head), jnp.bfloat16)
    payload = jax.ShapeDtypeStruct((chips, rows, 3 * head), jnp.bfloat16)

    def query_block(t):
        return (t + first if first else jnp.minimum(t, early - 1), 0, 0)

    return pl.pallas_call(
        kernel,
        grid=(chips - first,),
        out_shape=[payload] + [shape for shape, _ in more_out] + [grads, grads],
        in_specs=[
            SCALAR,
            pl.BlockSpec((1, rows, 4 * head), lambda t: (t + first, 0, 0)),
            pl.BlockSpec((chips, rows, 2 * head), lambda t: (0, 0, 2), pipeline_mode=pl.Buffered(1)),
            WHOLE,
        ]
        + more_in,
        out_specs=[pl.BlockSpec((1, rows, 2 * head), query_block)]
        + [spec for _, spec in more_out]
        + [WHOLE, WHOLE],
        scratch_shapes=[pltpu.VMEM(shape, kind) for shape, kind in scratch],
        input_output_aliases={4: 0} if first else {},
        compiler_params=pltpu.CompilerParams(
            dimension_semantics=("arbitrary",), vmem_limit_bytes=vmem * 2**20
        ),
        cost_estimate=pl.CostEstimate(
            flops=2 * products * 112 * rows * rows * head,
            bytes_accessed=8 * 2**20,
            transcendentals=2 * 112 * rows * rows,
        ),
        name=name,
    )(*operands)


def value_gradients(parity, own, other):
    chips, rows, _ = own.shape
    span = WINDOW // rows
    head = HEAD_SIZE
    dk = jax.ShapeDtypeStruct((span, rows, head), jnp.float32)
    return attention_call(
        value_kernel,
        "value_gradients",
        (parity, own, own, other),
        0,
        [],
        [(dk, WHOLE)],
        [
            ((2 * chips, rows, head), jnp.bfloat16),
            ((span, rows, head), jnp.bfloat16),
            ((span, head, rows), jnp.bfloat16),
            ((2 * chips, rows, head), jnp.float32),
            ((span + 1, rows, 2 * rows), jnp.bfloat16),
            ((span, rows, 2 * rows), jnp.bfloat16),
            ((span, rows, 2 * rows), jnp.float32),
        ],
        4,
        28,
    )


def score_gradients(parity, own, other, payload, dk):
    chips, rows, _ = own.shape
    span = WINDOW // rows
    head = HEAD_SIZE
    return attention_call(
        score_kernel,
        "score_gradients",
        (parity, own, own, other, payload, dk),
        span // 2,
        [pl.BlockSpec(memory_space=pl.ANY), WHOLE],
        [],
        [
            ((2 * chips, rows, head), jnp.bfloat16),
            ((2 * chips, rows, head), jnp.bfloat16),
            ((2 * chips, head, rows), jnp.bfloat16),
            ((2 * chips, rows, head), jnp.float32),
            ((span + 1, rows, 2 * rows), jnp.bfloat16),
            ((span + 1, rows, 2 * rows), jnp.float32),
        ],
        8,
        60,
    )


def small_call(
    kernel,
    name,
    out_shape,
    scratch,
    flops,
    *operands,
    grid=None,
    in_specs=None,
    out_specs=None,
    kind=jnp.bfloat16,
    vmem=16,
    aliases=None,
    moved=None,
):
    kinds = [jax.ShapeDtypeStruct(shape, kind) for shape in out_shape]
    specs = {}
    if grid is not None:
        specs = {"grid": grid}
    if moved is None:
        moved = sum(2 * x.size for x in operands) + sum(2 * math.prod(s) for s in out_shape)
    return pl.pallas_call(
        kernel,
        out_shape=kinds,
        in_specs=in_specs if in_specs is not None else [WHOLE] * len(operands),
        out_specs=out_specs if out_specs is not None else [WHOLE] * len(kinds),
        scratch_shapes=scratch,
        compiler_params=pltpu.CompilerParams(vmem_limit_bytes=vmem * 2**20),
        cost_estimate=pl.CostEstimate(flops=flops, bytes_accessed=moved, transcendentals=0),
        name=name,
        input_output_aliases=aliases or {},
        **specs,
    )(*operands)


def pack_heads(queries, output_gradient, saved_keys, saved_values):
    heads = KEY_VALUE_HEADS

    def kernel(*refs):
        out_ref, at = refs[-1], 0
        for ref in refs[:-1]:
            wide = ref.shape[1] // heads
            for g in range(heads):
                out_ref[g, :, at : at + wide] = ref[:, g * wide : (g + 1) * wide]
            at += wide

    rows = queries.shape[0]
    arrays = (queries, output_gradient, saved_keys, saved_values)
    part = rows // 2
    total = sum(x.shape[1] for x in arrays) // heads
    (packed,) = small_call(
        kernel,
        "pack_heads",
        [(heads, rows, total)],
        [],
        0,
        *arrays,
        grid=(rows // part,),
        in_specs=[pl.BlockSpec((part, x.shape[1]), lambda r: (r, 0)) for x in arrays],
        out_specs=[pl.BlockSpec((heads, part, total), lambda r: (0, r, 0))],
        vmem=60,
    )
    return packed


def pack_scores(payload, mine, theirs):
    def kernel(_, mine_ref, theirs_ref, out_ref):
        out_ref[...] = add(mine_ref[...], theirs_ref[...])

    chips, rows, head = mine.shape
    part = chips // 2
    block = pl.BlockSpec((part, rows, head), lambda t: (t, 0, 0))
    (packed,) = small_call(
        kernel,
        "pack_scores",
        [payload.shape],
        [],
        0,
        payload,
        mine,
        theirs,
        grid=(chips // part,),
        in_specs=[pl.BlockSpec(memory_space=pl.ANY), block, block],
        out_specs=[pl.BlockSpec((part, rows, head), lambda t: (t, 0, 2))],
        vmem=60,
        aliases={0: 0},
    )
    return packed


def unpack_scores(back):
    def kernel(in_ref, dq_ref, dk_ref):
        for g in range(heads):
            dq_ref[:, g * 2 * head : (g + 1) * 2 * head] = in_ref[g, :, : 2 * head]
            dk_ref[:, g * head : (g + 1) * head] = in_ref[g, :, 2 * head :]

    heads, rows, width = back.shape
    head = HEAD_SIZE
    part = rows // 4
    widths = (2 * head * heads, head * heads)
    return small_call(
        kernel,
        "unpack_scores",
        [(rows, w) for w in widths],
        [],
        0,
        back,
        grid=(rows // part,),
        in_specs=[pl.BlockSpec((heads, part, width), lambda r: (0, r, 0))],
        out_specs=[pl.BlockSpec((part, w), lambda r: (r, 0)) for w in widths],
    )


def pack_values(mine, theirs):
    def kernel(mine_ref, theirs_ref, out_ref):
        for x in range(2):
            for y in range(2):
                total = add(mine_ref[x, y, 0], theirs_ref[x, y, 0])
                for to in range(4):
                    out_ref[to // 2, to % 2, 0, 2 * x + y] = total

    chips, rows, head = mine.shape
    split = (2, 2, 2, rows, head)
    (packed,) = small_call(
        kernel,
        "pack_values",
        [split[:3] + (4, rows, head)],
        [],
        0,
        mine.reshape(split),
        theirs.reshape(split),
        grid=(2,),
        in_specs=[pl.BlockSpec((2, 2, 1, rows, head), lambda p: (0, 0, p, 0, 0))] * 2,
        out_specs=[pl.BlockSpec((2, 2, 1, 4, rows, head), lambda p: (0, 0, p, 0, 0, 0))],
        vmem=16,
    )
    return packed.reshape(chips, 4, rows, head)


def turn_input(place, input_rows):
    rows, depth = input_rows.shape
    share = depth // 16
    wide = 2 * HEAD_SIZE

    def kernel(place_ref, in_ref, *refs):
        out_refs, turned_s = refs[:-1], refs[-1]
        for at in range(0, depth, wide):
            turned_s[at : at + wide] = jnp.transpose(in_ref[:, at : at + wide])
        for distance, out_ref in enumerate(out_refs):
            to = place_ref[0] ^ distance
            for core in range(2):
                for group in range(2):
                    high = to % 2 if group else to % 2 ^ core
                    low = place_ref[2] if group else 1 - place_ref[2]
                    for half in range(2):
                        x = to // 2
                        if core:
                            x = jnp.where(place_ref[3] == half, x, 1 - x)
                        index = (((x * 2 + high) * 2 + low) * 2 + core) * 2 + half
                        at = (core * 2 + half) * share // 2
                        piece = turned_s[pl.ds(pl.multiple_of(index * (share // 2), 16), share // 2)]
                        out_ref[group, at : at + share // 2] = piece

    return small_call(
        kernel,
        "turn_input",
        [(2, 2 * share, rows)] * 4,
        [pltpu.VMEM((depth, rows), jnp.bfloat16)],
        0,
        place,
        input_rows,
        in_specs=[SCALAR, WHOLE],
        vmem=60,
    )


def input_product(place, columns, back):
    members = len(columns)
    heads, _, rows, head = back.shape
    share = columns[0].shape[1] // 2

    def kernel(place_ref, *refs):
        column_refs, back_ref = refs[:members], refs[members]
        give_ref, keep_ref, value_ref, x_s, sems = refs[members + 1 :]

        @pl.when(pl.program_id(0) == 0)
        def _():
            copies = [
                pltpu.make_async_copy(ref, x_s.at[d], sems.at[d])
                for d, ref in enumerate(column_refs)
            ]
            for copy in copies:
                copy.start()
            for copy in copies:
                copy.wait()

        member, core = place_ref[0], place_ref[1]
        v = [
            jnp.concatenate([back_ref[0, member ^ d], back_ref[1, member ^ d]], axis=1)
            for d in range(members)
        ]
        value_ref[...] = v[0]
        v = jnp.concatenate(v, axis=0)
        for at in range(2):
            for out_ref, which_core in ((give_ref, 1 - core), (keep_ref, core)):
                part = pl.ds(pl.multiple_of(which_core * share, 16), share)
                x = jnp.concatenate([x_s[d, at, part] for d in range(members)], axis=1)
                out_ref[at] = dot(x, v, (1, 0)).astype(jnp.bfloat16)

    halves = pl.BlockSpec((2, share, 2 * head), lambda g: (0, 0, g))
    return small_call(
        kernel,
        "input_product",
        [(2, share, heads * head)] * 2 + [(rows, heads * head)],
        [
            pltpu.VMEM((members, 2, 2 * share, rows), jnp.bfloat16),
            pltpu.SemaphoreType.DMA((members,)),
        ],
        0,
        place,
        *columns,
        back,
        grid=(heads // 2,),
        in_specs=[SCALAR]
        + [pl.BlockSpec(memory_space=pltpu.HBM)] * members
        + [pl.BlockSpec((2, members, rows, head), lambda g: (g, 0, 0, 0))],
        out_specs=[halves, halves, pl.BlockSpec((rows, 2 * head), lambda g: (0, g))],
        vmem=28,
        moved=0,
    )


def add32(a, b):
    return a.astype(jnp.float32) + b.astype(jnp.float32)


def add(a, b):
    return add32(a, b).astype(jnp.bfloat16)


def cut_pieces(place, keep, got):
    def kernel(place_ref, keep_ref, got_ref, cross_other_ref, cross_own_ref, stay_ref, second_ref, own_ref):
        mirror = place_ref[3]
        cross_other_ref[...] = add(keep_ref[0, 1 - mirror], got_ref[0, 1 - mirror])
        cross_own_ref[...] = add(keep_ref[1, 1 - mirror], got_ref[1, 1 - mirror])
        stay_ref[...] = add(keep_ref[0, mirror], got_ref[0, mirror])
        second_ref[...] = add(keep_ref[1, 1], got_ref[1, 1])
        own_ref[...] = add(keep_ref[1, 0], got_ref[1, 0])

    return small_call(
        kernel,
        "cut_pieces",
        [keep.shape[2:]] * 5,
        [],
        0,
        place,
        keep,
        got,
        in_specs=[SCALAR, WHOLE, WHOLE],
        vmem=60,
    )


def finish(place, turn, pieces):
    def kernel(place_ref, turn_ref, own_ref, near_ref, near2_ref, far_ref, other_ref, out_ref):
        total = jnp.where(place_ref[3] == 0, own_ref[...], far_ref[...]).astype(jnp.float32)
        total = total + add32(near_ref[...], near2_ref[...]) + other_ref[...].astype(jnp.float32)
        out_ref[...] = dot(total.astype(jnp.bfloat16), turn_ref[...], (1, 0))

    own = pieces[0]
    (out,) = small_call(
        kernel,
        "finish",
        [own.shape],
        [],
        2 * own.size * own.shape[1],
        place,
        turn,
        *pieces,
        in_specs=[SCALAR] + [WHOLE] * 6,
        kind=jnp.float32,
    )
    return out


def hadamard(order_size):
    place = np.arange(order_size)
    both = place[:, None] & place[None, :]
    parity = np.zeros_like(both)
    for bit in range(order_size.bit_length() - 1):
        parity ^= both >> bit & 1
    return (1 - 2 * parity) / math.sqrt(order_size)


def body(queries, saved_keys, saved_values, output_gradient, layer_input, hadamard_signs):
    width = saved_keys.shape[3]
    head = HEAD_SIZE
    chips = lax.axis_size("ctx") // 2
    sections = lax.axis_size("section")
    ctx = lax.axis_index("ctx").astype(jnp.int32)
    section = lax.axis_index("section").astype(jnp.int32)
    mirror = lax.axis_index("mirror").astype(jnp.int32)
    core = ctx & 1
    same_core = [[2 * chip + c for chip in range(chips)] for c in range(2)]
    member = (ctx >> 3) * 2 + (ctx >> 2 & 1)
    place = jnp.stack([member, core, ctx >> 1 & 1, mirror])

    def across(block):
        return lax.all_to_all(block, "ctx", 0, 0, tiled=True, axis_index_groups=same_core)

    def swap(block, bits):
        return lax.ppermute(block, "ctx", [(i, i ^ bits) for i in range(2 * chips)])

    turned = turn_input(place, layer_input[0, 0])
    own = across(
        pack_heads(queries[0, 0], output_gradient[0, 0], saved_keys[0, 0], saved_values[0, 0])
    )
    own, *turned = lax.optimization_barrier((own, *turned))
    other = swap(own[:, :, 4 * head :], 1)
    parity = core.reshape(1)
    columns = turned[:1] + [swap(turned[d], (d & 1) * 4 + (d >> 1) * 8) for d in range(1, 4)]

    scores, dk, dv_mine, dv_theirs = value_gradients(parity, own, other)
    values = pack_values(dv_mine, swap(dv_theirs, 1))
    values, own, *columns = lax.optimization_barrier((values, own, *columns))
    values_back = across(values)

    scores, dk_mine, dk_theirs = score_gradients(parity, own, other, scores, dk)
    scores = pack_scores(scores, dk_mine, swap(dk_theirs, 1))
    values_back, scores = lax.optimization_barrier((values_back, scores))
    scores_back = across(scores)
    give, keep, value_gradient = input_product(place, columns, values_back)
    got = swap(give, 1)

    keep = keep.reshape(2, 2, -1, width)
    got = got.reshape(keep.shape)
    sections = lax.axis_size("section")
    cross_other, cross_own, stay_other, second_own, first_own = cut_pieces(place, keep, got)

    def routed(block, route, groups):
        axes = ("section", "ctx", "mirror")
        pairs = [
            ((s * 2 * chips + i) * 2 + m, (t * 2 * chips + (i ^ groups[i % 2])) * 2 + n)
            for (s, m), (t, n) in route
            for i in range(2 * chips)
        ]
        return lax.ppermute(block, axes, pairs)

    far = [((s, 1), (sections - 1 - s, 1)) for s in range(sections)]
    cross = [((s, 1), (sections - 1 - s, 0)) for s in range(sections)]
    cross += [((s, 0), (s, 1)) for s in range(sections)]
    near_other = routed(cross_other, cross, (2, 6 ^ 8))
    other = routed(stay_other, far + [((s, 0), (s, 0)) for s in range(sections)], (2, 6))
    cross_own, second_own, scores_back = lax.optimization_barrier((cross_own, second_own, scores_back))
    near_own = routed(cross_own, cross, (0, 8))
    far_own = routed(second_own, far, (0, 0))
    signs = lax.dynamic_index_in_dim(hadamard_signs, section, 0, keepdims=False)
    turn = jnp.asarray(hadamard(width), jnp.bfloat16) * signs.astype(jnp.bfloat16)[:, None]
    rotated = finish(
        place,
        turn,
        (first_own, near_other, near_own, far_own, other),
    )
    query_gradient, key_gradient = unpack_scores(scores_back)
    return (
        query_gradient[None, None],
        key_gradient[None, None],
        value_gradient[None, None],
        rotated[None],
    )


def solution(mesh):
    split = P("section", "mirror", "ctx", None)
    return jax.shard_map(
        body,
        mesh=mesh,
        in_specs=(split, split, split, split, split, P()),
        out_specs=(split, split, split, P("section", ("ctx", "mirror"), None)),
        check_vma=False,
    )
```
